32 devices in a mesh: fsdp: 4 (over x, core), ctx: 8 (over z, y).
Axes of the slice: x: 2, y: 2, z: 4, core: 2. Of those that a mesh axis runs over, the one named last changes fastest.
Arguments:
- tokens: bfloat16 [12, 2048, 1024], P('fsdp', 'ctx'), may hold values from -6 to 6
- seq_lengths: int32 [12, 4], P('fsdp'), may hold values from 1 to 1794, 2048 in all within a row
- attn_gain: bfloat16 [1024], P('fsdp'), may hold values from 0.099609375 to 1.8984375
- w_query: bfloat16 [1024, 2048], P('fsdp'), may hold values from -0.1875 to 0.1875
- w_key: bfloat16 [1024, 1024], P('fsdp'), may hold values from -0.1875 to 0.1875
- w_value: bfloat16 [1024, 1024], P('fsdp'), may hold values from -0.1875 to 0.1875
- query_gain: bfloat16 [128], P('fsdp'), may hold values from 0.099609375 to 1.8984375
- key_gain: bfloat16 [128], P('fsdp'), may hold values from 0.099609375 to 1.8984375
- w_output: bfloat16 [2048, 1024], P('fsdp'), may hold values from -0.75 to 0.75
- mlp_gain: bfloat16 [1024], P('fsdp'), may hold values from 0.099609375 to 1.8984375
- w_gate: bfloat16 [1024, 3072], P('fsdp'), may hold values from -0.1875 to 0.1875
- w_up: bfloat16 [1024, 3072], P('fsdp'), may hold values from -0.1875 to 0.1875
- w_down: bfloat16 [3072, 1024], P('fsdp'), may hold values from -0.109375 to 0.109375
- out_grad: bfloat16 [12, 2048, 1024], P('fsdp', 'ctx'), may hold values from -6 to 6
Outputs:
- output: bfloat16 [12, 2048, 1024], P('fsdp', 'ctx')
- token_grad: float32 [12, 2048, 1024], P('fsdp', 'ctx')
- grad_attn_gain: float32 [1024], P('fsdp')
- grad_query: float32 [1024, 2048], P('fsdp')
- grad_key: float32 [1024, 1024], P('fsdp')
- grad_value: float32 [1024, 1024], P('fsdp')
- grad_query_gain: float32 [128], P('fsdp')
- grad_key_gain: float32 [128], P('fsdp')
- grad_output: float32 [2048, 1024], P('fsdp')
- grad_mlp_gain: float32 [1024], P('fsdp')
- grad_gate: float32 [1024, 3072], P('fsdp')
- grad_up: float32 [1024, 3072], P('fsdp')
- grad_down: float32 [3072, 1024], P('fsdp')
The draws below stay inside these ranges and needn't reach their ends.
Inputs may be any that keep to these rules, and one draw needn't show every extreme that they name: `seq_lengths`: each row lists the lengths of the 4 sequences of one group in their order; a row sums to 2048, and its largest entry is exactly 1794.
All inputs are finite; a program needn't handle non-finite values.
Results may differ from the reference program's by a relative error of at most 0.02.
Values may be sent and summed in bfloat16 or wider, within the bound.
No kernel may reach another device: no remote copies, remote signals or barrier semaphores. Data moves between devices by JAX's collectives and lax.ppermute only.
A program may use at most 320 MiB of HBM per device.

```python
import math
from functools import partial
import jax
import jax.numpy as jnp
import numpy as np
from jax import lax

D = 1024
NH = 16
KVH = 8
HD = 128
FF = 3072
GROUP = 2048
SEQS = 4
QW = 2048
KVW = 1024
LONGEST = 1794
BATCH = 12
TOKENS = 24576


def levels(own_key, shape, cuts, low, high):
    def one(dim, shards_of):
        heights = jax.random.uniform(jax.random.fold_in(jax.random.fold_in(own_key, 6), dim), (shards_of,), jnp.float32, low / len(cuts), high / len(cuts))
        return jnp.repeat(jnp.exp(heights), shape[dim] // shards_of).reshape((-1,) + (1,) * (len(shape) - dim - 1))

    level = one(*cuts[0])
    for cut in cuts[1:]:
        level = level * one(*cut)
    return level


def split_up(count, total, reach, skew):
    loads = [(1 << 20) // math.isqrt(rank ** skew) + 1 for rank in range(2, count + 1)]
    spare, counts = total - reach - (count - 1), [1] * (count - 1)
    while spare > 0:
        candidates = [i for i in range(count - 1) if counts[i] < reach]
        whole, budget = sum([loads[i] for i in candidates]), spare
        for i in candidates:
            extra = min(reach - counts[i], max(1, budget * loads[i] // whole), spare)
            counts[i] = counts[i] + extra
            spare = spare - extra
    return np.array([reach] + counts)


def uneven(rng, amount, total, reach, lean):
    if amount == 2:
        one = jax.random.randint(rng, (), max(1, total - reach), min(reach, total - 1) + 1)
        return jnp.stack([one, total - one])
    sizes = jnp.asarray(split_up(amount, total, reach, lean), jnp.int32)
    pairs = (amount - 1) // 2
    source_of, sink = sizes[1:1 + 2 * pairs:2], sizes[2:2 + 2 * pairs:2]
    slack = jnp.minimum(source_of - 1, reach - sink)
    passed = jax.random.randint(jax.random.fold_in(rng, 1), (pairs,), 0, 1 << 20) % (slack + 1)
    sizes = sizes.at[1:1 + 2 * pairs:2].set(source_of - passed).at[2:2 + 2 * pairs:2].set(sink + passed)
    return sizes[jax.random.permutation(jax.random.fold_in(rng, 2), amount)]


def centred(rng, extent, deviation, most, pieces=(), kind=jnp.bfloat16):
    values = jax.random.normal(rng, extent, jnp.float32) * deviation
    if len(pieces) > 0:
        values = levels(rng, extent, pieces, -0.22, 0.18) * values
    return jnp.clip(values, min=-most, max=most).astype(kind)


def setup_inputs(seed: int = 0) -> dict:
    splits = jax.random.split(jax.random.key(seed), 15)
    return {
        "tokens": centred(splits[0], (BATCH, GROUP, D), 1.0, 6.0, ((0, 4), (1, 8))),
        "seq_lengths": jax.vmap(lambda own: uneven(own, SEQS, GROUP, LONGEST, 0))(jax.random.split(splits[1], BATCH)).reshape((BATCH, SEQS)).astype(jnp.int32),
        "attn_gain": jnp.clip(1.0 + 0.18 * jax.random.normal(splits[2], (D,), jnp.float32), 0.099609375, 1.8984375).astype(jnp.bfloat16),
        "w_query": centred(splits[3], (D, QW), D ** -0.5, 0.1875, ((0, 4),)),
        "w_key": centred(splits[4], (D, KVW), D ** -0.5, 0.1875, ((0, 4),)),
        "w_value": centred(splits[5], (D, KVW), D ** -0.5, 0.1875, ((0, 4),)),
        "query_gain": jnp.clip(1.0 + 0.18 * jax.random.normal(splits[6], (HD,), jnp.float32), 0.099609375, 1.8984375).astype(jnp.bfloat16),
        "key_gain": jnp.clip(1.0 + 0.18 * jax.random.normal(splits[7], (HD,), jnp.float32), 0.099609375, 1.8984375).astype(jnp.bfloat16),
        "w_output": centred(splits[8], (QW, D), (QW // 32) ** -0.5, 0.75, ((0, 4),)),
        "mlp_gain": jnp.clip(1.0 + 0.18 * jax.random.normal(splits[9], (D,), jnp.float32), 0.099609375, 1.8984375).astype(jnp.bfloat16),
        "w_gate": centred(splits[10], (D, FF), D ** -0.5, 0.1875, ((0, 4),)),
        "w_up": centred(splits[11], (D, FF), D ** -0.5, 0.1875, ((0, 4),)),
        "w_down": centred(splits[12], (FF, D), FF ** -0.5, 0.109375, ((0, 4),)),
        "out_grad": centred(splits[13], (BATCH, GROUP, D), 1.0, 6.0, ((0, 4), (1, 8))),
    }


@jax.custom_vjp
def low(v):
    return lax.optimization_barrier(v.astype(jnp.bfloat16)).astype(jnp.float32)

@jax.custom_vjp
def low_back(v):
    return v

def low_keep(v):
    return (low(v), None)

def low_pass(kept, grad):
    return (grad,)

def back_keep(v):
    return (v, None)

def back_low(kept, grad):
    return (low(grad),)
low.defvjp(low_keep, low_pass)
low_back.defvjp(back_keep, back_low)
EPSILON = 1e-06
NEGATIVE = -1e+30
HIGHEST = lax.Precision.HIGHEST

def rms_gain(values, gain):
    return values * lax.rsqrt(lax.optimization_barrier(jnp.mean(values * values, axis=-1, keepdims=True)) + EPSILON) * gain

def rope_tables(positions, width):
    half_width = width // 2
    inverse = jnp.exp(jnp.arange(half_width, dtype=jnp.float32) * (-2.0 * math.log(1000000.0) / width))
    angles = positions.astype(jnp.float32)[:, None] * inverse[None, :]
    return (jnp.cos(angles), jnp.sin(angles))

def rotate(values, cosine, sine):
    half_width = values.shape[-1] // 2
    leading = values[..., :half_width]
    trailing = values[..., half_width:]
    cos_rows = cosine[:, None, :]
    sin_rows = sine[:, None, :]
    return jnp.concatenate([leading * cos_rows - trailing * sin_rows, trailing * cos_rows + leading * sin_rows], axis=-1)

def norm_rope(linear, gain, cosine, sine):
    width = gain.shape[0]
    shaped = linear.reshape(linear.shape[0], linear.shape[1] // width, width)
    return rotate(rms_gain(shaped, gain), cosine, sine).reshape(linear.shape)

def layout(lengths, places):
    ends = jnp.cumsum(lengths).astype(jnp.int32)
    starts = (ends - lengths).astype(jnp.int32)
    member = lax.optimization_barrier(jnp.sum((places[:, None] >= ends[None, :]).astype(jnp.int32), axis=1)).astype(jnp.int32)
    chosen = member[:, None] == jnp.arange(lengths.shape[0], dtype=jnp.int32)[None, :]
    return lax.optimization_barrier(jnp.sum(jnp.where(chosen, starts[None, :], 0), axis=1)).astype(jnp.int32)

def attend_rows(keys, values, item):
    queries, first, places = item
    scores = low_back(jnp.einsum('qkrd,pkd->krqp', queries, keys, precision=HIGHEST) * HD ** (-0.5))
    key_places = jnp.arange(keys.shape[0], dtype=jnp.int32)
    visible = (key_places[None, :] >= first[:, None]) & (key_places[None, :] <= places[:, None])
    scores = jnp.where(visible, scores, NEGATIVE)
    top = lax.optimization_barrier(jnp.max(scores, axis=-1, keepdims=True))
    expo = jnp.exp(scores - top)
    probs = low(expo / lax.optimization_barrier(jnp.sum(expo, axis=-1, keepdims=True)))
    return jnp.einsum('krqp,pkd->qkrd', probs, values, precision=HIGHEST)

def attend_group(item):
    queries, keys, values, first, places = item
    block = min(512, GROUP)
    count = GROUP // block
    shaped = (queries.reshape(count, block, KVH, NH // KVH, HD), first.reshape(count, block), places.reshape(count, block))
    result = lax.map(jax.checkpoint(partial(attend_rows, keys.reshape(GROUP, KVH, HD), values.reshape(GROUP, KVH, HD))), shaped)
    return result.reshape(GROUP, QW)

def layer(tokens, attn_gain, w_query, w_key, w_value, query_gain, key_gain, w_output, mlp_gain, w_gate, w_up, w_down, first, places, cosine, sine):
    flat = tokens.reshape(TOKENS, D)
    normed = low(rms_gain(flat, attn_gain))
    query_lin = low_back(jnp.dot(normed, w_query, precision=HIGHEST))
    key_lin = low_back(jnp.dot(normed, w_key, precision=HIGHEST))
    value_lin = low_back(jnp.dot(normed, w_value, precision=HIGHEST))
    queries = low(norm_rope(query_lin, query_gain, cosine, sine))
    keys = low(norm_rope(key_lin, key_gain, cosine, sine))
    values = low(value_lin)
    grouped = (queries.reshape(BATCH, GROUP, QW), keys.reshape(BATCH, GROUP, KVW), values.reshape(BATCH, GROUP, KVW), first, places)
    attended = lax.map(attend_group, grouped).reshape(TOKENS, QW)
    attended = low_back(low(attended))
    middle = flat + low_back(jnp.dot(attended, w_output, precision=HIGHEST))
    normed_mlp = low(rms_gain(middle, mlp_gain))
    gate = low_back(jnp.dot(normed_mlp, w_gate, precision=HIGHEST))
    upward = low_back(jnp.dot(normed_mlp, w_up, precision=HIGHEST))
    hidden = low(jax.nn.silu(gate) * upward)
    return (middle + low_back(jnp.dot(hidden, w_down, precision=HIGHEST))).reshape(BATCH, GROUP, D)

def reference(tokens, seq_lengths, attn_gain, w_query, w_key, w_value, query_gain, key_gain, w_output, mlp_gain, w_gate, w_up, w_down, out_grad):
    places = jnp.broadcast_to(jnp.arange(GROUP, dtype=jnp.int32)[None, :], (BATCH, GROUP))
    first = jax.vmap(layout)(seq_lengths, places)
    cosine, sine = rope_tables((places - first).reshape(TOKENS), HD)
    floats = [argument.astype(jnp.float32) for argument in (tokens, attn_gain, w_query, w_key, w_value, query_gain, key_gain, w_output, mlp_gain, w_gate, w_up, w_down)]

    def forward(*weights):
        return layer(*weights, first, places, cosine, sine)
    output, pullback = jax.vjp(forward, *floats)
    grads = pullback(out_grad.astype(jnp.float32))
    return (output.astype(jnp.bfloat16), grads[0], grads[1], grads[2], grads[3], grads[4], grads[5], grads[6], grads[7], grads[8], grads[9], grads[10], grads[11])
```

```python
import functools
import math

import jax
import jax.numpy as jnp
from jax import lax
from jax.experimental import pallas as pl
from jax.experimental.pallas import tpu as pltpu
from jax.sharding import PartitionSpec as P

HD = 128
EPSILON = 1e-06
SCALE = HD ** (-0.5)
LOG2E = math.log2(math.e)
BLOCK = 512
VMEM_LIMIT = 48 * 1024 * 1024
bf16 = jnp.bfloat16
f32 = jnp.float32


def matmul(left, right):
    return jnp.dot(left, right, preferred_element_type=f32)


def contract_rows(left, right):
    return lax.dot_general(left, right, (((0,), (0,)), ((), ())), preferred_element_type=f32)


def contract_cols(left, right):
    return lax.dot_general(left, right, (((1,), (1,)), ((), ())), preferred_element_type=f32)


def inverse_rms(values):
    return lax.rsqrt(jnp.mean(values * values, axis=-1, keepdims=True) + EPSILON)


def rms_backward(values, gain, grad):
    inverse = inverse_rms(values)
    scaled = grad * gain
    mean = jnp.mean(scaled * values, axis=-1, keepdims=True)
    return inverse * scaled - values * (inverse * inverse * inverse * mean)


def swiglu(gate, upward):
    return jax.nn.silu(gate) * upward


def rope(values, cosine, sine):
    return values * cosine + pltpu.roll(values, HD // 2, 1) * sine


def rope_back(grad, cosine, sine):
    return grad * cosine + pltpu.roll(grad * sine, HD // 2, 1)


def visible(first, row, column, size):
    key_places = row * size + lax.broadcasted_iota(jnp.int32, (size, size), 0)
    shown = key_places >= first
    if row == column:
        places = column * size + lax.broadcasted_iota(jnp.int32, (size, size), 1)
        shown = shown & (key_places <= places)
    return shown


def forward_kernel(
    lin_ref, cos_ref, sin_ref, first_ref, gain_ref, qkv_ref, att_ref, att_t_ref, lse_ref, k_scr, vt_scr
):
    step = pl.program_id(0)
    total = lin_ref.shape[0]
    size = min(BLOCK, total)

    @pl.when(step == 1)
    def store_values():
        values = lin_ref[...]
        qkv_ref[...] = values.astype(bf16)
        vt_scr[...] = values.T.astype(bf16)

    @pl.when(step != 1)
    def store_rotated():
        gain = jnp.where(step == 0, gain_ref[1:2, :], gain_ref[0:1, :])
        linear = lin_ref[...]
        normed = linear * inverse_rms(linear) * gain
        qkv_ref[...] = rope(normed, cos_ref[...], sin_ref[...]).astype(bf16)

    @pl.when(step == 0)
    def keep_keys():
        k_scr[...] = qkv_ref[...]

    @pl.when(step >= 2)
    def attend():
        for i in range(total // size):
            cols = slice(i * size, (i + 1) * size)
            queries = qkv_ref[cols, :]
            first = first_ref[:, cols]
            weight = jnp.zeros((1, size), f32)
            acc = jnp.zeros((HD, size), f32)
            for j in range(i + 1):
                rows = slice(j * size, (j + 1) * size)
                scores = contract_cols(k_scr[rows, :], queries) * (SCALE * LOG2E)
                probs = jnp.where(visible(first, j, i, size), jnp.exp2(scores), 0.0)
                weight = weight + jnp.sum(probs, axis=0, keepdims=True)
                acc = acc + matmul(vt_scr[:, rows], probs.astype(bf16))
            acc = acc * (1.0 / weight)
            att_t_ref[0, :, cols] = acc
            att_ref[cols, :] = acc.T.astype(bf16)
            lse_ref[0, :, cols] = jnp.log2(weight)


def attention_forward(lin, cosine, sine, first, gains):
    total, width = lin.shape
    heads = width // HD - 2
    last = heads + 2

    def column(t):
        return (0, jnp.where(t < 2, heads + t, t - 2))

    def query_column(t):
        return (0, jnp.maximum(t - 2, 0))

    full = lambda shape: pl.BlockSpec(shape, lambda t: (0,) * len(shape))
    return pl.pallas_call(
        forward_kernel,
        grid=(last,),
        out_shape=(
            jax.ShapeDtypeStruct((total, width), bf16),
            jax.ShapeDtypeStruct((total, heads * HD), bf16),
            jax.ShapeDtypeStruct((heads, HD, total), f32),
            jax.ShapeDtypeStruct((heads, 1, total), f32),
        ),
        in_specs=[
            pl.BlockSpec((total, HD), column),
            full((total, HD)),
            full((total, HD)),
            full((1, total)),
            full((2, HD)),
        ],
        out_specs=(
            pl.BlockSpec((total, HD), column),
            pl.BlockSpec((total, HD), query_column),
            pl.BlockSpec((1, HD, total), lambda t: (jnp.maximum(t - 2, 0), 0, 0)),
            pl.BlockSpec((1, 1, total), lambda t: (jnp.maximum(t - 2, 0), 0, 0)),
        ),
        scratch_shapes=[pltpu.VMEM((total, HD), bf16), pltpu.VMEM((HD, total), bf16)],
        compiler_params=pltpu.CompilerParams(vmem_limit_bytes=VMEM_LIMIT),
        cost_estimate=pl.CostEstimate(
            flops=heads * total * total * HD * 4,
            bytes_accessed=total * width * 12,
            transcendentals=heads * total * total // 2,
        ),
        name="attention_forward",
    )(lin, cosine, sine, first, gains)


def backward_kernel(
    q_ref,
    k_ref,
    v_ref,
    lin_ref,
    do_ref,
    att_t_ref,
    lse_ref,
    cos_ref,
    sin_ref,
    first_ref,
    gain_ref,
    out_ref,
    q_gain_ref,
    k_gain_ref,
    kt_scr,
    dk_scr,
    dv_scr,
):
    step = pl.program_id(0)
    heads = pl.num_programs(0) - 2
    total = q_ref.shape[0]
    size = min(BLOCK, total)

    @pl.when(step == 0)
    def clear():
        kt_scr[...] = k_ref[...].astype(f32).T.astype(bf16)
        dk_scr[...] = jnp.zeros_like(dk_scr)
        dv_scr[...] = jnp.zeros_like(dv_scr)
        q_gain_ref[...] = jnp.zeros_like(q_gain_ref)

    def norm_back(grad, rows, gain):
        turned = rope_back(grad, cos_ref[rows, :], sin_ref[rows, :])
        linear = lin_ref[rows, :]
        inverse = inverse_rms(linear)
        gain_part = jnp.sum(turned * (linear * inverse), axis=0, keepdims=True)
        scaled = turned * gain
        mean = jnp.mean(scaled * linear, axis=-1, keepdims=True)
        out_ref[rows, :] = (
            inverse * scaled - linear * (inverse * inverse * inverse * mean)
        ).astype(bf16)
        return gain_part

    @pl.when(step < heads)
    def head():
        for i in range(total // size):
            cols = slice(i * size, (i + 1) * size)
            queries = q_ref[cols, :]
            grads = do_ref[cols, :]
            delta = jnp.sum(grads.astype(f32).T * att_t_ref[0, :, cols], axis=0, keepdims=True)
            first = first_ref[:, cols]
            lse = lse_ref[0, :, cols]
            acc = jnp.zeros((HD, size), f32)
            for j in range(i + 1):
                rows = slice(j * size, (j + 1) * size)
                scores = contract_cols(k_ref[rows, :], queries) * (SCALE * LOG2E)
                probs = jnp.where(visible(first, j, i, size), jnp.exp2(scores - lse), 0.0)
                grad_probs = contract_cols(v_ref[rows, :], grads)
                grad_scores = (probs * (grad_probs - delta)).astype(bf16)
                dv_scr[rows, :] += matmul(probs.astype(bf16), grads)
                dk_scr[rows, :] += matmul(grad_scores, queries)
                acc = acc + matmul(kt_scr[:, rows], grad_scores)
            q_gain_ref[...] += norm_back((acc * SCALE).T, cols, gain_ref[0:1, :])

    @pl.when(step == heads)
    def keys():
        part = jnp.zeros((1, HD), f32)
        for i in range(total // size):
            rows = slice(i * size, (i + 1) * size)
            part = part + norm_back(dk_scr[rows, :] * SCALE, rows, gain_ref[1:2, :])
        k_gain_ref[...] = part

    @pl.when(step == heads + 1)
    def values():
        out_ref[...] = dv_scr[...].astype(bf16)


def attention_backward(qkv, lin, grad, att_t, lse, cosine, sine, first, gains):
    total, width = lin.shape
    heads = width // HD - 2
    last = heads + 2

    def query_column(t):
        return (0, jnp.minimum(t, heads - 1))

    full = lambda shape: pl.BlockSpec(shape, lambda t: (0,) * len(shape))
    return pl.pallas_call(
        backward_kernel,
        grid=(last,),
        out_shape=(
            jax.ShapeDtypeStruct((total, width), bf16),
            jax.ShapeDtypeStruct((1, HD), f32),
            jax.ShapeDtypeStruct((1, HD), f32),
        ),
        in_specs=[
            pl.BlockSpec((total, HD), query_column),
            pl.BlockSpec((total, HD), lambda t: (0, heads)),
            pl.BlockSpec((total, HD), lambda t: (0, heads + 1)),
            pl.BlockSpec((total, HD), lambda t: (0, jnp.minimum(t, heads))),
            pl.BlockSpec((total, HD), query_column),
            pl.BlockSpec((1, HD, total), lambda t: (jnp.minimum(t, heads - 1), 0, 0)),
            pl.BlockSpec((1, 1, total), lambda t: (jnp.minimum(t, heads - 1), 0, 0)),
            full((total, HD)),
            full((total, HD)),
            full((1, total)),
            full((2, HD)),
        ],
        out_specs=(
            pl.BlockSpec((total, HD), lambda t: (0, t)),
            full((1, HD)),
            full((1, HD)),
        ),
        scratch_shapes=[
            pltpu.VMEM((HD, total), bf16),
            pltpu.VMEM((total, HD), f32),
            pltpu.VMEM((total, HD), f32),
        ],
        compiler_params=pltpu.CompilerParams(vmem_limit_bytes=VMEM_LIMIT),
        cost_estimate=pl.CostEstimate(
            flops=heads * total * total * HD * 10,
            bytes_accessed=total * width * 12,
            transcendentals=heads * total * total // 2,
        ),
        name="attention_backward",
    )(qkv, qkv, qkv, lin, grad, att_t, lse, cosine, sine, first, gains)


class Ring:
    def __init__(self, axis, count):
        self.axis = axis
        self.count = count
        order = [0, 2, 4, 6, 7, 5, 3, 1] if count == 8 else list(range(count))
        place = [order.index(k) for k in range(count)]
        self.order = jnp.asarray(order, jnp.int32)
        self.me = jnp.asarray(place, jnp.int32)[lax.axis_index(axis)]
        self.right = [(order[k], order[(k + 1) % count]) for k in range(count)]
        self.left = [(b, a) for a, b in self.right]

    def go_right(self, value):
        return lax.ppermute(value, self.axis, self.right)

    def go_left(self, value):
        return lax.ppermute(value, self.axis, self.left)

    def member(self, offset):
        return self.order[lax.rem(self.me + offset + 2 * self.count, self.count)]

    def gather(self, block, out_type=None):
        count, rows = self.count, block.shape[0]
        half = rows // 2
        out_type = out_type or block.dtype
        out = jnp.zeros((count * rows,) + block.shape[1:], out_type)
        zeros = (0,) * (block.ndim - 1)

        def put(out, value, offset, shift=0):
            start = self.member(offset) * rows + shift
            return lax.dynamic_update_slice(out, value.astype(out_type), (start,) + zeros)

        out = put(out, block, 0)
        right = left = block
        stages = []
        for hop in range(1, (count - 1) // 2 + 1):
            right, left = self.go_right(right), self.go_left(left)
            stages.append(right)
            out = put(out, right, -hop)
            out = put(out, left, hop)
        if count % 2 == 0:
            far = count // 2
            out = put(out, self.go_right(right[:half]), -far)
            out = put(out, self.go_left(left[half:]), far, half)
        return out, stages[-1]

    def scatter_sum(self, blocks):
        count, rows = self.count, blocks.shape[1]
        half = rows // 2
        zeros = (0,) * (blocks.ndim - 2)
        sizes = (1, half) + blocks.shape[2:]

        def pick(offset, shift):
            return lax.dynamic_slice(blocks, (self.member(offset), shift) + zeros, sizes)[0]

        right, left = pick(-1, 0), pick(1, half)
        for hop in range(1, count):
            right, left = self.go_right(right), self.go_left(left)
            right = right.astype(f32) + pick(-1 - hop, 0).astype(f32)
            left = left.astype(f32) + pick(1 + hop, half).astype(f32)
            if hop < count - 1:
                right, left = right.astype(bf16), left.astype(bf16)
        return right, left

    def sum_all(self, shard):
        rows = shard.shape[0] // self.count
        blocks = shard.reshape((self.count, rows) + shard.shape[1:])
        halves = [part.astype(bf16) for part in self.scatter_sum(blocks)]
        return self.gather(jnp.concatenate(halves, axis=0), f32)[0]


class Cube:
    def __init__(self, axis, count):
        self.axis = axis
        self.count = count
        self.me = lax.axis_index(axis)
        self.bits = [1 << k for k in range(count.bit_length() - 1)]

    def swap(self, value, bit):
        return lax.ppermute(value, self.axis, [(k, k ^ bit) for k in range(self.count)])

    def gather(self, shard):
        held = {0: shard}
        for bit in reversed(self.bits):
            held.update({key ^ bit: self.swap(value, bit) for key, value in held.items()})
        rows = shard.shape[0]
        out = jnp.zeros((self.count * rows,) + shard.shape[1:], shard.dtype)
        zeros = (0,) * (shard.ndim - 1)
        for key, value in held.items():
            out = lax.dynamic_update_slice(out, value, ((self.me ^ key) * rows,) + zeros)
        return out

    def scatter_sum(self, whole):
        rows = whole.shape[0] // self.count
        zeros = (0,) * (whole.ndim - 1)
        sizes = (rows,) + whole.shape[1:]
        held = {
            key: lax.dynamic_slice(whole, ((self.me ^ key) * rows,) + zeros, sizes)
            for key in range(self.count)
        }
        for bit in self.bits:
            for key in [key for key in held if key & bit]:
                arrived = self.swap(held.pop(key), bit)
                kept = key ^ bit
                held[kept] = (held[kept].astype(f32) + arrived.astype(f32)).astype(bf16)
        return held[0]


def layout(lengths, places):
    ends = jnp.cumsum(lengths)
    starts = ends - lengths
    member = jnp.sum((places[:, None] >= ends[None, :]).astype(jnp.int32), axis=1)
    chosen = member[:, None] == jnp.arange(lengths.shape[0], dtype=jnp.int32)[None, :]
    return jnp.sum(jnp.where(chosen, starts[None, :], 0), axis=1)


def body(
    fsdp_count,
    ctx_count,
    tokens,
    seq_lengths,
    attn_gain,
    w_query,
    w_key,
    w_value,
    query_gain,
    key_gain,
    w_output,
    mlp_gain,
    w_gate,
    w_up,
    w_down,
    out_grad,
):
    groups, rows, width = tokens.shape
    total = rows * ctx_count
    flat_rows = groups * rows
    ctx = lax.axis_index("ctx")
    ring, cube = Ring("ctx", ctx_count), Cube("fsdp", fsdp_count)

    query_heads, key_heads = w_query.shape[1] // HD, w_key.shape[1] // HD
    heads = query_heads // ctx_count
    query_width = heads * HD
    shared = ctx_count // key_heads
    key_head = ctx // shared
    w_mine = jnp.concatenate(
        [
            lax.dynamic_slice(w_query, (0, ctx * query_width), (w_query.shape[0], query_width)),
            lax.dynamic_slice(w_key, (0, key_head * HD), (w_key.shape[0], HD)),
            lax.dynamic_slice(w_value, (0, key_head * HD), (w_value.shape[0], HD)),
        ],
        axis=1,
    )
    packed = jnp.concatenate([attn_gain, mlp_gain, query_gain, key_gain])
    all_gains = cube.gather(packed[None, :]).astype(f32)
    d_shard, h_shard = attn_gain.shape[0], query_gain.shape[0]
    gain_attn = all_gains[:, :d_shard].reshape(-1)
    gain_mlp = all_gains[:, d_shard : 2 * d_shard].reshape(-1)
    gain_query = all_gains[:, 2 * d_shard : 2 * d_shard + h_shard].reshape(-1)
    gain_key = all_gains[:, 2 * d_shard + h_shard :].reshape(-1)
    head_gains = jnp.stack([gain_query, gain_key])
    w_heads = cube.gather(w_mine)

    full_output = lax.all_gather(w_output, "fsdp", axis=0, tiled=True)
    full_gate = lax.all_gather(w_gate, "fsdp", axis=0, tiled=True)
    full_up = lax.all_gather(w_up, "fsdp", axis=0, tiled=True)
    full_down = lax.all_gather(w_down, "fsdp", axis=0, tiled=True)

    places = jnp.arange(total, dtype=jnp.int32)
    first = jax.vmap(lambda lengths: layout(lengths, places))(seq_lengths)
    lane = jnp.arange(HD, dtype=jnp.int32)
    inverse = jnp.exp(
        lax.rem(lane, HD // 2).astype(f32) * (-2.0 * math.log(1000000.0) / HD)
    )
    angles = (places[None, :] - first).astype(f32)[:, :, None] * inverse[None, None, :]
    cosine = jnp.cos(angles)
    sine = jnp.sin(angles) * jnp.where(lane < HD // 2, -1.0, 1.0)

    tag = None
    group_normed, group_lin, saved, attended = [], [], [], []
    for g in range(groups):
        block = tokens[g]
        if tag is not None:
            block, tag = lax.optimization_barrier((block, tag))
        all_tokens, tag = ring.gather(block)
        values = all_tokens.astype(f32)
        normed = (values * inverse_rms(values) * gain_attn).astype(bf16)
        lin = matmul(normed, w_heads)
        qkv, att, att_t, lse = attention_forward(
            lin, cosine[g], sine[g], first[g][None, :], head_gains
        )
        back = lax.all_to_all(
            att.reshape(ctx_count, rows, query_width), "ctx", 0, 0, tiled=True
        )
        attended.append(jnp.swapaxes(back, 0, 1).reshape(rows, ctx_count * query_width))
        group_normed.append(normed)
        group_lin.append(lin)
        saved.append((qkv, att_t, lse))
    attended_low = jnp.concatenate(attended, axis=0)

    inputs = tokens.reshape(flat_rows, width).astype(f32)
    cotangent = out_grad.reshape(flat_rows, width)
    middle = inputs + matmul(attended_low, full_output)
    normed_mlp = (middle * inverse_rms(middle) * gain_mlp).astype(bf16)
    gate = matmul(normed_mlp, full_gate)
    upward = matmul(normed_mlp, full_up)
    hidden, swiglu_back = jax.vjp(swiglu, gate, upward)
    hidden = hidden.astype(bf16)
    output = (middle + matmul(hidden, full_down)).astype(bf16)
    grad_down = contract_rows(hidden, cotangent).astype(bf16)
    grad_gate_lin, grad_up_lin = swiglu_back(contract_cols(cotangent, full_down))
    grad_gate_low = grad_gate_lin.astype(bf16)
    grad_up_low = grad_up_lin.astype(bf16)
    grad_normed_mlp = contract_cols(grad_gate_low, full_gate) + contract_cols(grad_up_low, full_up)
    grad_middle = cotangent.astype(f32) + rms_backward(middle, gain_mlp, grad_normed_mlp)
    grad_branch = grad_middle.astype(bf16)
    grad_attended = contract_cols(grad_branch, full_output).astype(bf16)
    grad_gate = contract_rows(normed_mlp, grad_gate_low).astype(bf16)
    grad_up = contract_rows(normed_mlp, grad_up_low).astype(bf16)
    grad_output = contract_rows(attended_low, grad_branch).astype(bf16)

    grad_heads = jnp.zeros(w_heads.shape, f32)
    grad_query_gain = jnp.zeros((1, HD), f32)
    grad_key_gain = jnp.zeros((1, HD), f32)
    token_grads = []
    for g in range(groups):
        part = grad_attended[g * rows : (g + 1) * rows].reshape(rows, ctx_count, query_width)
        grad_att = lax.all_to_all(jnp.swapaxes(part, 0, 1), "ctx", 0, 0, tiled=True)
        qkv, att_t, lse = saved[g]
        grad_low, query_part, key_part = attention_backward(
            qkv,
            group_lin[g],
            grad_att.reshape(total, query_width),
            att_t,
            lse,
            cosine[g],
            sine[g],
            first[g][None, :],
            head_gains,
        )
        grad_query_gain = grad_query_gain + query_part
        grad_key_gain = grad_key_gain + key_part
        partial = contract_cols(grad_low, w_heads).astype(bf16)
        halves = ring.scatter_sum(partial.reshape(ctx_count, rows, width))
        grad_heads = grad_heads + contract_rows(group_normed[g], grad_low)
        grad_normed = jnp.concatenate(halves, axis=0)
        chosen = slice(g * rows, (g + 1) * rows)
        token_grads.append(
            grad_middle[chosen] + rms_backward(inputs[chosen], gain_attn, grad_normed)
        )
    token_grad = jnp.stack(token_grads)

    shard_down, shard_gate, shard_up, shard_output = [
        ring.sum_all(cube.scatter_sum(value))
        for value in (grad_down, grad_gate, grad_up, grad_output)
    ]
    small = jnp.concatenate(
        [grad_query_gain.reshape(fsdp_count, h_shard), grad_key_gain.reshape(fsdp_count, h_shard)],
        axis=1,
    )
    small = jnp.pad(small, ((0, 0), (0, d_shard - 2 * h_shard))).reshape(-1, 1)
    small = jnp.pad(small, ((0, 0), (0, HD - 1)))
    mine = cube.scatter_sum(jnp.concatenate([grad_heads, small], axis=1).astype(bf16))
    gathered, ignored = ring.gather(mine[None], f32)
    shard_query = jnp.swapaxes(gathered[:, :, :query_width], 0, 1).reshape(d_shard, -1)

    def key_columns(start):
        part = gathered[:, :, start : start + HD].reshape(key_heads, shared, d_shard, HD)
        return jnp.swapaxes(jnp.sum(part, axis=1), 0, 1).reshape(d_shard, -1)

    shard_key = key_columns(query_width)
    shard_value = key_columns(query_width + HD)
    head_sums = jnp.sum(gathered[:, : 2 * h_shard, query_width + 2 * HD], axis=0)
    shard_attn_gain = (
        jnp.sum(shard_query * w_query.astype(f32), axis=1)
        + jnp.sum(shard_key * w_key.astype(f32), axis=1)
        + jnp.sum(shard_value * w_value.astype(f32), axis=1)
    ) / attn_gain.astype(f32)
    shard_mlp_gain = (
        jnp.sum(shard_gate * w_gate.astype(f32), axis=1)
        + jnp.sum(shard_up * w_up.astype(f32), axis=1)
    ) / mlp_gain.astype(f32)
    return (
        output.reshape(groups, rows, width),
        token_grad,
        shard_attn_gain,
        shard_query,
        shard_key,
        shard_value,
        head_sums[:h_shard],
        head_sums[h_shard:],
        shard_output,
        shard_mlp_gain,
        shard_gate,
        shard_up,
        shard_down,
    )


def solution(mesh):
    rows, matrix, vector = P("fsdp", "ctx", None), P("fsdp", None), P("fsdp")
    return jax.shard_map(
        functools.partial(body, mesh.shape["fsdp"], mesh.shape["ctx"]),
        mesh=mesh,
        in_specs=(
            rows,
            matrix,
            vector,
            matrix,
            matrix,
            matrix,
            vector,
            vector,
            matrix,
            vector,
            matrix,
            matrix,
            matrix,
            rows,
        ),
        out_specs=(
            rows,
            rows,
            vector,
            matrix,
            matrix,
            matrix,
            vector,
            vector,
            matrix,
            vector,
            matrix,
            matrix,
            matrix,
        ),
        check_vma=False,
    )
```

```python
import functools
import math

import jax
import jax.numpy as jnp
from jax import lax
from jax.experimental import pallas as pl
from jax.experimental.pallas import tpu as pltpu
from jax.sharding import PartitionSpec as P

HD = 128
EPSILON = 1e-06
SCALE = HD ** (-0.5)
LOG2E = math.log2(math.e)
BLOCK = 512
FEED_BLOCK = 512
VMEM_LIMIT = 48 * 1024 * 1024
bf16 = jnp.bfloat16
f32 = jnp.float32


def matmul(left, right):
    return jnp.dot(left, right, preferred_element_type=f32)


def contract_rows(left, right):
    return lax.dot_general(left, right, (((0,), (0,)), ((), ())), preferred_element_type=f32)


def contract_cols(left, right):
    return lax.dot_general(left, right, (((1,), (1,)), ((), ())), preferred_element_type=f32)


def inverse_rms(values):
    return lax.rsqrt(jnp.mean(values * values, axis=-1, keepdims=True) + EPSILON)


def rms_backward(values, gain, grad):
    inverse = inverse_rms(values)
    scaled = grad * gain
    mean = jnp.mean(scaled * values, axis=-1, keepdims=True)
    return inverse * scaled - values * (inverse * inverse * inverse * mean)


def rope(values, cosine, sine):
    return values * cosine + pltpu.roll(values, HD // 2, 1) * sine


def rope_back(grad, cosine, sine):
    return grad * cosine + pltpu.roll(grad * sine, HD // 2, 1)


def visible(first, row, column, size):
    key_places = row * size + lax.broadcasted_iota(jnp.int32, (size, size), 0)
    shown = key_places >= first
    if row == column:
        places = column * size + lax.broadcasted_iota(jnp.int32, (size, size), 1)
        shown = shown & (key_places <= places)
    return shown


def forward_kernel(
    lin_ref, cos_ref, sin_ref, first_ref, gain_ref, qkv_ref, att_ref, att_t_ref, lse_ref, k_scr, vt_scr
):
    step = pl.program_id(0)
    total = lin_ref.shape[0]
    size = min(BLOCK, total)

    @pl.when(step == 1)
    def store_values():
        values = lin_ref[...]
        qkv_ref[...] = values.astype(bf16)
        vt_scr[...] = values.T.astype(bf16)

    @pl.when(step != 1)
    def store_rotated():
        gain = jnp.where(step == 0, gain_ref[1:2, :], gain_ref[0:1, :])
        linear = lin_ref[...]
        normed = linear * inverse_rms(linear) * gain
        qkv_ref[...] = rope(normed, cos_ref[...], sin_ref[...]).astype(bf16)

    @pl.when(step == 0)
    def keep_keys():
        k_scr[...] = qkv_ref[...]

    @pl.when(step >= 2)
    def attend():
        for i in range(total // size):
            cols = slice(i * size, (i + 1) * size)
            queries = qkv_ref[cols, :]
            first = first_ref[:, cols]
            weight = jnp.zeros((1, size), f32)
            acc = jnp.zeros((HD, size), f32)
            for j in range(i + 1):
                rows = slice(j * size, (j + 1) * size)
                scores = contract_cols(k_scr[rows, :], queries) * (SCALE * LOG2E)
                probs = jnp.where(visible(first, j, i, size), jnp.exp2(scores), 0.0)
                weight = weight + jnp.sum(probs, axis=0, keepdims=True)
                acc = acc + matmul(vt_scr[:, rows], probs.astype(bf16))
            acc = acc * (1.0 / weight)
            att_t_ref[0, :, cols] = acc
            att_ref[cols, :] = acc.T.astype(bf16)
            lse_ref[0, :, cols] = jnp.log2(weight)


def attention_forward(lin, cosine, sine, first, gains):
    total, width = lin.shape
    heads = width // HD - 2
    last = heads + 2

    def column(t):
        return (0, jnp.where(t < 2, heads + t, t - 2))

    def query_column(t):
        return (0, jnp.maximum(t - 2, 0))

    full = lambda shape: pl.BlockSpec(shape, lambda t: (0,) * len(shape))
    return pl.pallas_call(
        forward_kernel,
        grid=(last,),
        out_shape=(
            jax.ShapeDtypeStruct((total, width), bf16),
            jax.ShapeDtypeStruct((total, heads * HD), bf16),
            jax.ShapeDtypeStruct((heads, HD, total), f32),
            jax.ShapeDtypeStruct((heads, 1, total), f32),
        ),
        in_specs=[
            pl.BlockSpec((total, HD), column),
            full((total, HD)),
            full((total, HD)),
            full((1, total)),
            full((2, HD)),
        ],
        out_specs=(
            pl.BlockSpec((total, HD), column),
            pl.BlockSpec((total, HD), query_column),
            pl.BlockSpec((1, HD, total), lambda t: (jnp.maximum(t - 2, 0), 0, 0)),
            pl.BlockSpec((1, 1, total), lambda t: (jnp.maximum(t - 2, 0), 0, 0)),
        ),
        scratch_shapes=[pltpu.VMEM((total, HD), bf16), pltpu.VMEM((HD, total), bf16)],
        compiler_params=pltpu.CompilerParams(vmem_limit_bytes=VMEM_LIMIT),
        cost_estimate=pl.CostEstimate(
            flops=heads * total * total * HD * 4,
            bytes_accessed=total * width * 12,
            transcendentals=heads * total * total // 2,
        ),
        name="attention_forward",
    )(lin, cosine, sine, first, gains)


def backward_kernel(
    q_ref,
    k_ref,
    v_ref,
    lin_ref,
    do_ref,
    att_t_ref,
    lse_ref,
    cos_ref,
    sin_ref,
    first_ref,
    gain_ref,
    out_ref,
    q_gain_ref,
    k_gain_ref,
    kt_scr,
    dk_scr,
    dv_scr,
):
    step = pl.program_id(0)
    heads = pl.num_programs(0) - 2
    total = q_ref.shape[0]
    size = min(BLOCK, total)

    @pl.when(step == 0)
    def clear():
        kt_scr[...] = k_ref[...].astype(f32).T.astype(bf16)
        dk_scr[...] = jnp.zeros_like(dk_scr)
        dv_scr[...] = jnp.zeros_like(dv_scr)
        q_gain_ref[...] = jnp.zeros_like(q_gain_ref)

    def norm_back(grad, rows, gain):
        turned = rope_back(grad, cos_ref[rows, :], sin_ref[rows, :])
        linear = lin_ref[rows, :]
        inverse = inverse_rms(linear)
        gain_part = jnp.sum(turned * (linear * inverse), axis=0, keepdims=True)
        scaled = turned * gain
        mean = jnp.mean(scaled * linear, axis=-1, keepdims=True)
        out_ref[rows, :] = (
            inverse * scaled - linear * (inverse * inverse * inverse * mean)
        ).astype(bf16)
        return gain_part

    @pl.when(step < heads)
    def head():
        for i in range(total // size):
            cols = slice(i * size, (i + 1) * size)
            queries = q_ref[cols, :]
            grads = do_ref[cols, :]
            delta = jnp.sum(grads.astype(f32).T * att_t_ref[0, :, cols], axis=0, keepdims=True)
            first = first_ref[:, cols]
            lse = lse_ref[0, :, cols]
            acc = jnp.zeros((HD, size), f32)
            for j in range(i + 1):
                rows = slice(j * size, (j + 1) * size)
                scores = contract_cols(k_ref[rows, :], queries) * (SCALE * LOG2E)
                probs = jnp.where(visible(first, j, i, size), jnp.exp2(scores - lse), 0.0)
                grad_probs = contract_cols(v_ref[rows, :], grads)
                grad_scores = (probs * (grad_probs - delta)).astype(bf16)
                dv_scr[rows, :] += matmul(probs.astype(bf16), grads)
                dk_scr[rows, :] += matmul(grad_scores, queries)
                acc = acc + matmul(kt_scr[:, rows], grad_scores)
            q_gain_ref[...] += norm_back((acc * SCALE).T, cols, gain_ref[0:1, :])

    @pl.when(step == heads)
    def keys():
        part = jnp.zeros((1, HD), f32)
        for i in range(total // size):
            rows = slice(i * size, (i + 1) * size)
            part = part + norm_back(dk_scr[rows, :] * SCALE, rows, gain_ref[1:2, :])
        k_gain_ref[...] = part

    @pl.when(step == heads + 1)
    def values():
        out_ref[...] = dv_scr[...].astype(bf16)


def attention_backward(qkv, lin, grad, att_t, lse, cosine, sine, first, gains):
    total, width = lin.shape
    heads = width // HD - 2
    last = heads + 2

    def query_column(t):
        return (0, jnp.minimum(t, heads - 1))

    full = lambda shape: pl.BlockSpec(shape, lambda t: (0,) * len(shape))
    return pl.pallas_call(
        backward_kernel,
        grid=(last,),
        out_shape=(
            jax.ShapeDtypeStruct((total, width), bf16),
            jax.ShapeDtypeStruct((1, HD), f32),
            jax.ShapeDtypeStruct((1, HD), f32),
        ),
        in_specs=[
            pl.BlockSpec((total, HD), query_column),
            pl.BlockSpec((total, HD), lambda t: (0, heads)),
            pl.BlockSpec((total, HD), lambda t: (0, heads + 1)),
            pl.BlockSpec((total, HD), lambda t: (0, jnp.minimum(t, heads))),
            pl.BlockSpec((total, HD), query_column),
            pl.BlockSpec((1, HD, total), lambda t: (jnp.minimum(t, heads - 1), 0, 0)),
            pl.BlockSpec((1, 1, total), lambda t: (jnp.minimum(t, heads - 1), 0, 0)),
            full((total, HD)),
            full((total, HD)),
            full((1, total)),
            full((2, HD)),
        ],
        out_specs=(
            pl.BlockSpec((total, HD), lambda t: (0, t)),
            full((1, HD)),
            full((1, HD)),
        ),
        scratch_shapes=[
            pltpu.VMEM((HD, total), bf16),
            pltpu.VMEM((total, HD), f32),
            pltpu.VMEM((total, HD), f32),
        ],
        compiler_params=pltpu.CompilerParams(vmem_limit_bytes=VMEM_LIMIT),
        cost_estimate=pl.CostEstimate(
            flops=heads * total * total * HD * 10,
            bytes_accessed=total * width * 12,
            transcendentals=heads * total * total // 2,
        ),
        name="attention_backward",
    )(qkv, qkv, qkv, lin, grad, att_t, lse, cosine, sine, first, gains)


def feed_kernel(
    x_ref, cot_ref, gate_ref, up_ref, down_ref, hid_ref, grad_gate_ref, grad_up_ref, out_ref, back_ref
):
    step = pl.program_id(0)
    total = x_ref.shape[0]
    size = 256 if total % 256 == 0 else 128

    @pl.when(step == 0)
    def clear():
        out_ref[...] = jnp.zeros_like(out_ref)
        back_ref[...] = jnp.zeros_like(back_ref)

    for i in range(total // size):
        rows = slice(i * size, (i + 1) * size)
        gate = matmul(x_ref[rows, :], gate_ref[...])
        upward = matmul(x_ref[rows, :], up_ref[...])
        grad_hidden = contract_cols(cot_ref[rows, :], down_ref[...])
        sigmoid = 1.0 / (1.0 + jnp.exp(-gate))
        activated = gate * sigmoid
        hidden = (activated * upward).astype(bf16)
        hid_ref[rows, :] = hidden
        slope = sigmoid * (1.0 + gate * (1.0 - sigmoid))
        grad_gate = (grad_hidden * upward * slope).astype(bf16)
        grad_up = (grad_hidden * activated).astype(bf16)
        grad_gate_ref[rows, :] = grad_gate
        grad_up_ref[rows, :] = grad_up
        out_ref[rows, :] += matmul(hidden, down_ref[...])
        back_ref[rows, :] += contract_cols(grad_gate, gate_ref[...]) + contract_cols(
            grad_up, up_ref[...]
        )


def feed_forward(normed, cotangent, gate, up, down):
    total, width = normed.shape
    hidden_width = down.shape[0]
    block = min(FEED_BLOCK, hidden_width)
    whole = pl.BlockSpec((total, width), lambda t: (0, 0))
    return pl.pallas_call(
        feed_kernel,
        grid=(hidden_width // block,),
        out_shape=(
            jax.ShapeDtypeStruct((total, hidden_width), bf16),
            jax.ShapeDtypeStruct((total, hidden_width), bf16),
            jax.ShapeDtypeStruct((total, hidden_width), bf16),
            jax.ShapeDtypeStruct((total, width), f32),
            jax.ShapeDtypeStruct((total, width), f32),
        ),
        in_specs=[
            whole,
            whole,
            pl.BlockSpec((width, block), lambda t: (0, t)),
            pl.BlockSpec((width, block), lambda t: (0, t)),
            pl.BlockSpec((block, width), lambda t: (t, 0)),
        ],
        out_specs=(
            pl.BlockSpec((total, block), lambda t: (0, t)),
            pl.BlockSpec((total, block), lambda t: (0, t)),
            pl.BlockSpec((total, block), lambda t: (0, t)),
            whole,
            whole,
        ),
        compiler_params=pltpu.CompilerParams(vmem_limit_bytes=VMEM_LIMIT),
        cost_estimate=pl.CostEstimate(
            flops=total * width * hidden_width * 12,
            bytes_accessed=hidden_width * (6 * width + 6 * total) + total * width * 12,
            transcendentals=total * hidden_width,
        ),
        name="feed_forward",
    )(normed, cotangent, gate, up, down)


def table_row(table, number):
    table = jnp.asarray(table, jnp.int32)
    row = lax.dynamic_slice(
        table, (number, 0), (1, table.shape[1]), allow_negative_indices=False
    )[0]
    return [row[k] for k in range(table.shape[1])]


class Ring:
    def __init__(self, axis, count):
        self.axis = axis
        self.count = count
        order = [0, 2, 4, 6, 7, 5, 3, 1] if count == 8 else list(range(count))
        place = [order.index(k) for k in range(count)]
        self.members = table_row(
            [[order[(place[k] + hop) % count] for hop in range(count)] for k in range(count)],
            lax.axis_index(axis),
        )
        self.right = [(order[k], order[(k + 1) % count]) for k in range(count)]
        self.left = [(b, a) for a, b in self.right]

    def go_right(self, value):
        return lax.ppermute(value, self.axis, self.right)

    def go_left(self, value):
        return lax.ppermute(value, self.axis, self.left)

    def member(self, offset):
        return self.members[offset % self.count]

    def gather(self, block, axis=0, out_type=None):
        count, rows = self.count, block.shape[axis]
        half = rows // 2
        out_type = out_type or block.dtype
        shape = list(block.shape)
        shape[axis] = count * rows
        out = jnp.zeros(shape, out_type)

        def put(out, value, offset, shift=0):
            start = [0] * block.ndim
            start[axis] = self.member(offset) * rows + shift
            return lax.dynamic_update_slice(
                out, value.astype(out_type), start, allow_negative_indices=False
            )

        right = left = block
        put_next = [(block, 0, 0)]
        for hop in range(1, (count - 1) // 2 + 1):
            right, left = yield right, left
            for item in put_next:
                out = put(out, *item)
            right, left, out = lax.optimization_barrier((right, left, out))
            put_next = [(right, -hop, 0), (left, hop, 0)]
        if count % 2 == 0:
            far = count // 2
            near_half = lax.slice_in_dim(right, 0, half, axis=axis)
            far_half = lax.slice_in_dim(left, half, rows, axis=axis)
            right, left = yield near_half, far_half
            put_next += [(right, -far, 0), (left, far, half)]
        for item in put_next:
            out = put(out, *item)
        return out

    def scatter_sum(self, whole, axis=0):
        rows = whole.shape[axis] // self.count
        half = rows // 2
        shape = list(whole.shape)
        blocks = whole.reshape(shape[:axis] + [self.count, rows] + shape[axis + 1 :])
        sizes = shape[:axis] + [1, half] + shape[axis + 1 :]

        def pick(offset, shift):
            start = [0] * blocks.ndim
            start[axis], start[axis + 1] = self.member(offset), shift
            value = lax.dynamic_slice(blocks, start, sizes, allow_negative_indices=False)
            return jnp.squeeze(value, axis)

        right, left = pick(-1, 0), pick(1, half)
        for hop in range(1, self.count):
            right, left = yield right, left
            right = right.astype(f32) + pick(-1 - hop, 0).astype(f32)
            left = left.astype(f32) + pick(1 + hop, half).astype(f32)
            if hop < self.count - 1:
                right, left = right.astype(bf16), left.astype(bf16)
        return right, left

    def sum_all(self, shard):
        halves = yield from self.scatter_sum(shard)
        block = jnp.concatenate([part.astype(bf16) for part in halves], axis=0)
        return (yield from self.gather(block, out_type=f32))

    def run(self, chains):
        results, arrived, token = {}, {}, None
        number = 0
        while len(results) < len(chains):
            for k, (start, steps) in enumerate(chains):
                if k in results or number < start:
                    continue
                try:
                    payload = steps.send(arrived.get(k))
                except StopIteration as stop:
                    results[k] = stop.value
                    continue
                if token is not None:
                    payload, token = lax.optimization_barrier((payload, token))
                token = payload[0]
                arrived[k] = (self.go_right(payload[0]), self.go_left(payload[1]))
            number += 1
        return [results[k] for k in range(len(chains))]


class Cube:
    def __init__(self, axis, count):
        self.axis = axis
        self.count = count
        self.members = table_row(
            [[k ^ key for key in range(count)] for k in range(count)], lax.axis_index(axis)
        )
        self.bits = [1 << k for k in range(count.bit_length() - 1)]

    def swap(self, value, bit):
        return lax.ppermute(value, self.axis, [(k, k ^ bit) for k in range(self.count)])

    def gather(self, shard):
        held = {0: shard}
        for bit in reversed(self.bits):
            held.update({key ^ bit: self.swap(value, bit) for key, value in held.items()})
        rows = shard.shape[0]
        out = jnp.zeros((self.count * rows,) + shard.shape[1:], shard.dtype)
        for key, value in held.items():
            start = (self.members[key] * rows,) + (0,) * (shard.ndim - 1)
            out = lax.dynamic_update_slice(out, value, start, allow_negative_indices=False)
        return out

    def scatter_sum(self, whole):
        blocks = whole.reshape((self.count, whole.shape[0] // self.count) + whole.shape[1:])
        held = {
            key: lax.dynamic_slice(
                blocks,
                (self.members[key],) + (0,) * whole.ndim,
                (1,) + blocks.shape[1:],
                allow_negative_indices=False,
            )[0]
            for key in range(self.count)
        }
        for bit in self.bits:
            far = [key for key in held if key & bit]
            arrived = yield bit, [held.pop(key) for key in far]
            for key, value in zip(far, arrived):
                kept = key ^ bit
                held[kept] = (held[kept].astype(f32) + value.astype(f32)).astype(bf16)
        return held[0]

    def send(self, payload):
        bit, values = payload
        return [self.swap(value, bit) for value in values]

    def finish(self, steps, arrived=None):
        while True:
            try:
                arrived = self.send(steps.send(arrived))
            except StopIteration as stop:
                return stop.value


def layout(lengths, places):
    ends = jnp.cumsum(lengths)
    starts = ends - lengths
    member = jnp.sum((places[:, None] >= ends[None, :]).astype(jnp.int32), axis=1)
    chosen = member[:, None] == jnp.arange(lengths.shape[0], dtype=jnp.int32)[None, :]
    return jnp.sum(jnp.where(chosen, starts[None, :], 0), axis=1)


def body(
    fsdp_count,
    ctx_count,
    tokens,
    seq_lengths,
    attn_gain,
    w_query,
    w_key,
    w_value,
    query_gain,
    key_gain,
    w_output,
    mlp_gain,
    w_gate,
    w_up,
    w_down,
    out_grad,
):
    groups, rows, width = tokens.shape
    total = rows * ctx_count
    flat_rows = groups * rows
    ctx = lax.axis_index("ctx")
    ring, cube = Ring("ctx", ctx_count), Cube("fsdp", fsdp_count)

    query_heads, key_heads = w_query.shape[1] // HD, w_key.shape[1] // HD
    heads = query_heads // ctx_count
    query_width = heads * HD
    shared = ctx_count // key_heads
    key_head = ctx // shared
    w_mine = jnp.concatenate(
        [
            lax.dynamic_slice(w_query, (0, ctx * query_width), (w_query.shape[0], query_width)),
            lax.dynamic_slice(w_key, (0, key_head * HD), (w_key.shape[0], HD)),
            lax.dynamic_slice(w_value, (0, key_head * HD), (w_value.shape[0], HD)),
        ],
        axis=1,
    )
    packed = jnp.concatenate([attn_gain, mlp_gain, query_gain, key_gain])
    all_gains = cube.gather(packed[None, :]).astype(f32)
    d_shard, h_shard = attn_gain.shape[0], query_gain.shape[0]
    gain_attn = all_gains[:, :d_shard].reshape(-1)
    gain_mlp = all_gains[:, d_shard : 2 * d_shard].reshape(-1)
    gain_query = all_gains[:, 2 * d_shard : 2 * d_shard + h_shard].reshape(-1)
    gain_key = all_gains[:, 2 * d_shard + h_shard :].reshape(-1)
    head_gains = jnp.stack([gain_query, gain_key])
    w_heads = cube.gather(w_mine)

    full_output = lax.all_gather(w_output, "fsdp", axis=0, tiled=True)
    full_gate = lax.all_gather(w_gate, "fsdp", axis=0, tiled=True)
    full_up = lax.all_gather(w_up, "fsdp", axis=0, tiled=True)
    full_down = lax.all_gather(w_down, "fsdp", axis=0, tiled=True)

    places = jnp.arange(total, dtype=jnp.int32)
    first = jax.vmap(lambda lengths: layout(lengths, places))(seq_lengths)
    lane = jnp.arange(HD, dtype=jnp.int32)
    inverse = jnp.exp(
        lax.rem(lane, HD // 2).astype(f32) * (-2.0 * math.log(1000000.0) / HD)
    )
    angles = (places[None, :] - first).astype(f32)[:, :, None] * inverse[None, None, :]
    cosine = jnp.cos(angles)
    sine = jnp.sin(angles) * jnp.where(lane < HD // 2, -1.0, 1.0)

    (all_tokens,) = ring.run([(0, ring.gather(tokens, axis=1))])
    group_normed, group_lin, saved, attended = [], [], [], []
    for g in range(groups):
        values = all_tokens[g].astype(f32)
        normed = (values * inverse_rms(values) * gain_attn).astype(bf16)
        lin = matmul(normed, w_heads)
        qkv, att, att_t, lse = attention_forward(
            lin, cosine[g], sine[g], first[g][None, :], head_gains
        )
        back = lax.all_to_all(
            att.reshape(ctx_count, rows, query_width), "ctx", 0, 0, tiled=True
        )
        attended.append(jnp.swapaxes(back, 0, 1).reshape(rows, ctx_count * query_width))
        group_normed.append(normed)
        group_lin.append(lin)
        saved.append((qkv, att_t, lse))

    attended_low = jnp.concatenate(attended, axis=0)

    inputs = tokens.reshape(flat_rows, width).astype(f32)
    cotangent = out_grad.reshape(flat_rows, width)
    middle = inputs + matmul(attended_low, full_output)
    normed_mlp = (middle * inverse_rms(middle) * gain_mlp).astype(bf16)
    hidden, grad_gate_low, grad_up_low, feed_out, grad_normed_mlp = feed_forward(
        normed_mlp, cotangent, full_gate, full_up, full_down
    )
    grad_middle = cotangent.astype(f32) + rms_backward(middle, gain_mlp, grad_normed_mlp)
    grad_branch = grad_middle.astype(bf16)
    group_grad, part = [], None
    for g in range(groups):
        branch = grad_branch[g * rows : (g + 1) * rows]
        if part is not None:
            branch, part = lax.optimization_barrier((branch, part))
        part = contract_cols(branch, full_output).astype(bf16)
        part = jnp.swapaxes(part.reshape(rows, ctx_count, query_width), 0, 1)
        arrived = lax.all_to_all(part, "ctx", 0, 0, tiled=True)
        group_grad.append(arrived.reshape(total, query_width))
    hidden, normed_mlp, grad_gate_low, grad_up_low, attended_low, grad_branch, feed_out, part = (
        lax.optimization_barrier(
            (
                hidden,
                normed_mlp,
                grad_gate_low,
                grad_up_low,
                attended_low,
                grad_branch,
                feed_out,
                part,
            )
        )
    )
    output = (middle + feed_out).astype(bf16)
    weight_steps = [
        cube.scatter_sum(contract_rows(left, right).astype(bf16))
        for left, right in (
            (hidden, cotangent),
            (attended_low, grad_branch),
            (normed_mlp, grad_gate_low),
            (normed_mlp, grad_up_low),
        )
    ]

    grad_heads = jnp.zeros(w_heads.shape, f32)
    grad_query_gain = jnp.zeros((1, HD), f32)
    grad_key_gain = jnp.zeros((1, HD), f32)
    group_low, partials = [], []
    order = ((2, 3, 0, 1, 2, 3), (0, 1), (2,))
    weight_sums = [None] * len(weight_steps)
    weight_arrived = [None] * len(weight_steps)
    for g in range(groups):
        qkv, att_t, lse = saved[g]
        for k in order[min(g, 2)] if g < 3 else ():
            if weight_sums[k] is not None:
                continue
            try:
                bit, values = weight_steps[k].send(weight_arrived[k])
            except StopIteration as stop:
                tied = stop.value
                tied, group_grad[g] = lax.optimization_barrier((tied, group_grad[g]))
                weight_sums[k] = tied
                continue
            values, group_grad[g] = lax.optimization_barrier((values, group_grad[g]))
            weight_arrived[k] = cube.send((bit, values))
        grad_low, query_part, key_part = attention_backward(
            qkv,
            group_lin[g],
            group_grad[g],
            att_t,
            lse,
            cosine[g],
            sine[g],
            first[g][None, :],
            head_gains,
        )
        grad_query_gain = grad_query_gain + query_part
        grad_key_gain = grad_key_gain + key_part
        group_low.append(grad_low)
        partial = contract_cols(grad_low, w_heads).astype(bf16)
        if g + 1 < groups:
            group_grad[g + 1], partial = lax.optimization_barrier((group_grad[g + 1], partial))
        partials.append(partial)
    for k, steps in enumerate(weight_steps):
        if weight_sums[k] is None:
            weight_sums[k] = cube.finish(steps, weight_arrived[k])
    shard_down, shard_output, shard_gate, shard_up = weight_sums
    for g in range(groups):
        grad_heads = grad_heads + contract_rows(group_normed[g], group_low[g])
    first_part = jnp.stack(partials[:-1])
    last_part = partials[-1]

    small = jnp.concatenate(
        [grad_query_gain.reshape(fsdp_count, h_shard), grad_key_gain.reshape(fsdp_count, h_shard)],
        axis=1,
    )
    small = jnp.pad(small, ((0, 0), (0, d_shard - 2 * h_shard))).reshape(-1, 1)
    small = jnp.pad(small, ((0, 0), (0, HD - 1)))
    mine = cube.finish(
        cube.scatter_sum(jnp.concatenate([grad_heads, small], axis=1).astype(bf16))
    )
    split = shard_down.shape[0]
    shard_rows = jnp.concatenate([shard_down, shard_output], axis=0)
    shard_pair = jnp.concatenate([shard_gate, shard_up], axis=0)
    first_halves, summed_rows, last_halves, summed_pair, gathered = ring.run(
        [
            (0, ring.scatter_sum(first_part, axis=1)),
            (3, ring.sum_all(shard_rows)),
            (0, ring.scatter_sum(last_part)),
            (1, ring.sum_all(shard_pair)),
            (5, ring.gather(mine, out_type=f32)),
        ]
    )
    grad_normed = jnp.concatenate(
        [jnp.concatenate(first_halves, axis=1), jnp.concatenate(last_halves, axis=0)[None]], axis=0
    ).reshape(flat_rows, width)
    token_grad = grad_middle + rms_backward(inputs, gain_attn, grad_normed)
    shard_down, shard_output = summed_rows[:split], summed_rows[split:]
    shard_gate, shard_up = summed_pair[:d_shard], summed_pair[d_shard:]
    gathered = gathered.reshape(ctx_count, d_shard, -1)
    shard_query = jnp.swapaxes(gathered[:, :, :query_width], 0, 1).reshape(d_shard, -1)

    def key_columns(start):
        part = gathered[:, :, start : start + HD].reshape(key_heads, shared, d_shard, HD)
        return jnp.swapaxes(jnp.sum(part, axis=1), 0, 1).reshape(d_shard, -1)

    shard_key = key_columns(query_width)
    shard_value = key_columns(query_width + HD)
    head_sums = jnp.sum(gathered[:, : 2 * h_shard, query_width + 2 * HD], axis=0)
    shard_attn_gain = (
        jnp.sum(shard_query * w_query.astype(f32), axis=1)
        + jnp.sum(shard_key * w_key.astype(f32), axis=1)
        + jnp.sum(shard_value * w_value.astype(f32), axis=1)
    ) / attn_gain.astype(f32)
    shard_mlp_gain = (
        jnp.sum(shard_gate * w_gate.astype(f32), axis=1)
        + jnp.sum(shard_up * w_up.astype(f32), axis=1)
    ) / mlp_gain.astype(f32)
    return (
        output.reshape(groups, rows, width),
        token_grad.reshape(groups, rows, width),
        shard_attn_gain,
        shard_query,
        shard_key,
        shard_value,
        head_sums[:h_shard],
        head_sums[h_shard:],
        shard_output,
        shard_mlp_gain,
        shard_gate,
        shard_up,
        shard_down,
    )


def solution(mesh):
    rows, matrix, vector = P("fsdp", "ctx", None), P("fsdp", None), P("fsdp")
    return jax.shard_map(
        functools.partial(body, mesh.shape["fsdp"], mesh.shape["ctx"]),
        mesh=mesh,
        in_specs=(
            rows,
            matrix,
            vector,
            matrix,
            matrix,
            matrix,
            vector,
            vector,
            matrix,
            vector,
            matrix,
            matrix,
            matrix,
            rows,
        ),
        out_specs=(
            rows,
            rows,
            vector,
            matrix,
            matrix,
            matrix,
            vector,
            vector,
            matrix,
            vector,
            matrix,
            matrix,
            matrix,
        ),
        check_vma=False,
    )
```

```python
import functools
import math

import jax
import jax.numpy as jnp
from jax import lax
from jax.experimental import pallas as pl
from jax.experimental.pallas import tpu as pltpu
from jax.sharding import PartitionSpec as P

HD = 128
EPSILON = 1e-06
SCALE = HD ** (-0.5)
LOG2E = math.log2(math.e)
BLOCK = 512
FEED_BLOCK = 512
VMEM_LIMIT = 48 * 1024 * 1024
bf16 = jnp.bfloat16
f32 = jnp.float32


def matmul(left, right):
    return jnp.dot(left, right, preferred_element_type=f32)


def contract_rows(left, right):
    return lax.dot_general(left, right, (((0,), (0,)), ((), ())), preferred_element_type=f32)


def contract_cols(left, right):
    return lax.dot_general(left, right, (((1,), (1,)), ((), ())), preferred_element_type=f32)


def inverse_rms(values):
    return lax.rsqrt(jnp.mean(values * values, axis=-1, keepdims=True) + EPSILON)


def rms_backward(values, gain, grad):
    inverse = inverse_rms(values)
    scaled = grad * gain
    mean = jnp.mean(scaled * values, axis=-1, keepdims=True)
    return inverse * scaled - values * (inverse * inverse * inverse * mean)


def rope(values, cosine, sine):
    return values * cosine + pltpu.roll(values, HD // 2, 1) * sine


def rope_back(grad, cosine, sine):
    return grad * cosine + pltpu.roll(grad * sine, HD // 2, 1)


def visible(first, row, column, size):
    key_places = row * size + lax.broadcasted_iota(jnp.int32, (size, size), 0)
    shown = key_places >= first
    if row == column:
        places = column * size + lax.broadcasted_iota(jnp.int32, (size, size), 1)
        shown = shown & (key_places <= places)
    return shown


def forward_kernel(
    lin_ref, cos_ref, sin_ref, first_ref, gain_ref, qkv_ref, att_ref, att_t_ref, lse_ref, k_scr, vt_scr
):
    step = pl.program_id(0)
    total = lin_ref.shape[0]
    size = min(BLOCK, total)

    @pl.when(step == 1)
    def store_values():
        values = lin_ref[...]
        qkv_ref[...] = values.astype(bf16)
        vt_scr[...] = values.T.astype(bf16)

    @pl.when(step != 1)
    def store_rotated():
        gain = jnp.where(step == 0, gain_ref[1:2, :], gain_ref[0:1, :])
        linear = lin_ref[...]
        normed = linear * inverse_rms(linear) * gain
        qkv_ref[...] = rope(normed, cos_ref[...], sin_ref[...]).astype(bf16)

    @pl.when(step == 0)
    def keep_keys():
        k_scr[...] = qkv_ref[...]

    @pl.when(step >= 2)
    def attend():
        for i in range(total // size):
            cols = slice(i * size, (i + 1) * size)
            queries = qkv_ref[cols, :]
            first = first_ref[:, cols]
            weight = jnp.zeros((1, size), f32)
            acc = jnp.zeros((HD, size), f32)
            for j in range(i + 1):
                rows = slice(j * size, (j + 1) * size)
                scores = contract_cols(k_scr[rows, :], queries) * (SCALE * LOG2E)
                probs = jnp.where(visible(first, j, i, size), jnp.exp2(scores), 0.0)
                weight = weight + jnp.sum(probs, axis=0, keepdims=True)
                acc = acc + matmul(vt_scr[:, rows], probs.astype(bf16))
            acc = acc * (1.0 / weight)
            att_t_ref[0, :, cols] = acc
            att_ref[cols, :] = acc.T.astype(bf16)
            lse_ref[0, :, cols] = jnp.log2(weight)


def attention_forward(lin, cosine, sine, first, gains):
    total, width = lin.shape
    heads = width // HD - 2
    last = heads + 2

    def column(t):
        return (0, jnp.where(t < 2, heads + t, t - 2))

    def query_column(t):
        return (0, jnp.maximum(t - 2, 0))

    full = lambda shape: pl.BlockSpec(shape, lambda t: (0,) * len(shape))
    return pl.pallas_call(
        forward_kernel,
        grid=(last,),
        out_shape=(
            jax.ShapeDtypeStruct((total, width), bf16),
            jax.ShapeDtypeStruct((total, heads * HD), bf16),
            jax.ShapeDtypeStruct((heads, HD, total), f32),
            jax.ShapeDtypeStruct((heads, 1, total), f32),
        ),
        in_specs=[
            pl.BlockSpec((total, HD), column),
            full((total, HD)),
            full((total, HD)),
            full((1, total)),
            full((2, HD)),
        ],
        out_specs=(
            pl.BlockSpec((total, HD), column),
            pl.BlockSpec((total, HD), query_column),
            pl.BlockSpec((1, HD, total), lambda t: (jnp.maximum(t - 2, 0), 0, 0)),
            pl.BlockSpec((1, 1, total), lambda t: (jnp.maximum(t - 2, 0), 0, 0)),
        ),
        scratch_shapes=[pltpu.VMEM((total, HD), bf16), pltpu.VMEM((HD, total), bf16)],
        compiler_params=pltpu.CompilerParams(vmem_limit_bytes=VMEM_LIMIT),
        cost_estimate=pl.CostEstimate(
            flops=heads * total * total * HD * 4,
            bytes_accessed=total * width * 12,
            transcendentals=heads * total * total // 2,
        ),
        name="attention_forward",
    )(lin, cosine, sine, first, gains)


def backward_kernel(
    q_ref,
    k_ref,
    v_ref,
    lin_ref,
    do_ref,
    att_t_ref,
    lse_ref,
    cos_ref,
    sin_ref,
    first_ref,
    gain_ref,
    out_ref,
    q_gain_ref,
    k_gain_ref,
    kt_scr,
    dk_scr,
    dv_scr,
):
    step = pl.program_id(0)
    heads = pl.num_programs(0) - 2
    total = q_ref.shape[0]
    size = min(BLOCK, total)

    @pl.when(step == 0)
    def clear():
        kt_scr[...] = k_ref[...].astype(f32).T.astype(bf16)
        dk_scr[...] = jnp.zeros_like(dk_scr)
        dv_scr[...] = jnp.zeros_like(dv_scr)
        q_gain_ref[...] = jnp.zeros_like(q_gain_ref)

    def norm_back(grad, rows, gain):
        turned = rope_back(grad, cos_ref[rows, :], sin_ref[rows, :])
        linear = lin_ref[rows, :]
        inverse = inverse_rms(linear)
        gain_part = jnp.sum(turned * (linear * inverse), axis=0, keepdims=True)
        scaled = turned * gain
        mean = jnp.mean(scaled * linear, axis=-1, keepdims=True)
        out_ref[rows, :] = (
            inverse * scaled - linear * (inverse * inverse * inverse * mean)
        ).astype(bf16)
        return gain_part

    @pl.when(step < heads)
    def head():
        for i in range(total // size):
            cols = slice(i * size, (i + 1) * size)
            queries = q_ref[cols, :]
            grads = do_ref[cols, :]
            delta = jnp.sum(grads.astype(f32).T * att_t_ref[0, :, cols], axis=0, keepdims=True)
            first = first_ref[:, cols]
            lse = lse_ref[0, :, cols]
            acc = jnp.zeros((HD, size), f32)
            for j in range(i + 1):
                rows = slice(j * size, (j + 1) * size)
                scores = contract_cols(k_ref[rows, :], queries) * (SCALE * LOG2E)
                probs = jnp.where(visible(first, j, i, size), jnp.exp2(scores - lse), 0.0)
                grad_probs = contract_cols(v_ref[rows, :], grads)
                grad_scores = (probs * (grad_probs - delta)).astype(bf16)
                dv_scr[rows, :] += matmul(probs.astype(bf16), grads)
                dk_scr[rows, :] += matmul(grad_scores, queries)
                acc = acc + matmul(kt_scr[:, rows], grad_scores)
            q_gain_ref[...] += norm_back((acc * SCALE).T, cols, gain_ref[0:1, :])

    @pl.when(step == heads)
    def keys():
        part = jnp.zeros((1, HD), f32)
        for i in range(total // size):
            rows = slice(i * size, (i + 1) * size)
            part = part + norm_back(dk_scr[rows, :] * SCALE, rows, gain_ref[1:2, :])
        k_gain_ref[...] = part

    @pl.when(step == heads + 1)
    def values():
        out_ref[...] = dv_scr[...].astype(bf16)


def attention_backward(qkv, lin, grad, att_t, lse, cosine, sine, first, gains):
    total, width = lin.shape
    heads = width // HD - 2
    last = heads + 2

    def query_column(t):
        return (0, jnp.minimum(t, heads - 1))

    full = lambda shape: pl.BlockSpec(shape, lambda t: (0,) * len(shape))
    return pl.pallas_call(
        backward_kernel,
        grid=(last,),
        out_shape=(
            jax.ShapeDtypeStruct((total, width), bf16),
            jax.ShapeDtypeStruct((1, HD), f32),
            jax.ShapeDtypeStruct((1, HD), f32),
        ),
        in_specs=[
            pl.BlockSpec((total, HD), query_column),
            pl.BlockSpec((total, HD), lambda t: (0, heads)),
            pl.BlockSpec((total, HD), lambda t: (0, heads + 1)),
            pl.BlockSpec((total, HD), lambda t: (0, jnp.minimum(t, heads))),
            pl.BlockSpec((total, HD), query_column),
            pl.BlockSpec((1, HD, total), lambda t: (jnp.minimum(t, heads - 1), 0, 0)),
            pl.BlockSpec((1, 1, total), lambda t: (jnp.minimum(t, heads - 1), 0, 0)),
            full((total, HD)),
            full((total, HD)),
            full((1, total)),
            full((2, HD)),
        ],
        out_specs=(
            pl.BlockSpec((total, HD), lambda t: (0, t)),
            full((1, HD)),
            full((1, HD)),
        ),
        scratch_shapes=[
            pltpu.VMEM((HD, total), bf16),
            pltpu.VMEM((total, HD), f32),
            pltpu.VMEM((total, HD), f32),
        ],
        compiler_params=pltpu.CompilerParams(vmem_limit_bytes=VMEM_LIMIT),
        cost_estimate=pl.CostEstimate(
            flops=heads * total * total * HD * 10,
            bytes_accessed=total * width * 12,
            transcendentals=heads * total * total // 2,
        ),
        name="attention_backward",
    )(qkv, qkv, qkv, lin, grad, att_t, lse, cosine, sine, first, gains)


def feed_kernel(
    x_ref, cot_ref, gate_ref, up_ref, down_ref, hid_ref, grad_gate_ref, grad_up_ref, out_ref, back_ref
):
    step = pl.program_id(0)
    total = x_ref.shape[0]
    size = 256 if total % 256 == 0 else 128

    @pl.when(step == 0)
    def clear():
        out_ref[...] = jnp.zeros_like(out_ref)
        back_ref[...] = jnp.zeros_like(back_ref)

    for i in range(total // size):
        rows = slice(i * size, (i + 1) * size)
        gate = matmul(x_ref[rows, :], gate_ref[...])
        upward = matmul(x_ref[rows, :], up_ref[...])
        grad_hidden = contract_cols(cot_ref[rows, :], down_ref[...])
        sigmoid = 1.0 / (1.0 + jnp.exp(-gate))
        activated = gate * sigmoid
        hidden = (activated * upward).astype(bf16)
        hid_ref[rows, :] = hidden
        slope = sigmoid * (1.0 + gate * (1.0 - sigmoid))
        grad_gate = (grad_hidden * upward * slope).astype(bf16)
        grad_up = (grad_hidden * activated).astype(bf16)
        grad_gate_ref[rows, :] = grad_gate
        grad_up_ref[rows, :] = grad_up
        out_ref[rows, :] += matmul(hidden, down_ref[...])
        back_ref[rows, :] += contract_cols(grad_gate, gate_ref[...]) + contract_cols(
            grad_up, up_ref[...]
        )


def feed_forward(normed, cotangent, gate, up, down):
    total, width = normed.shape
    hidden_width = down.shape[0]
    block = min(FEED_BLOCK, hidden_width)
    whole = pl.BlockSpec((total, width), lambda t: (0, 0))
    return pl.pallas_call(
        feed_kernel,
        grid=(hidden_width // block,),
        out_shape=(
            jax.ShapeDtypeStruct((total, hidden_width), bf16),
            jax.ShapeDtypeStruct((total, hidden_width), bf16),
            jax.ShapeDtypeStruct((total, hidden_width), bf16),
            jax.ShapeDtypeStruct((total, width), f32),
            jax.ShapeDtypeStruct((total, width), f32),
        ),
        in_specs=[
            whole,
            whole,
            pl.BlockSpec((width, block), lambda t: (0, t)),
            pl.BlockSpec((width, block), lambda t: (0, t)),
            pl.BlockSpec((block, width), lambda t: (t, 0)),
        ],
        out_specs=(
            pl.BlockSpec((total, block), lambda t: (0, t)),
            pl.BlockSpec((total, block), lambda t: (0, t)),
            pl.BlockSpec((total, block), lambda t: (0, t)),
            whole,
            whole,
        ),
        compiler_params=pltpu.CompilerParams(vmem_limit_bytes=VMEM_LIMIT),
        cost_estimate=pl.CostEstimate(
            flops=total * width * hidden_width * 12,
            bytes_accessed=hidden_width * (6 * width + 6 * total) + total * width * 12,
            transcendentals=total * hidden_width,
        ),
        name="feed_forward",
    )(normed, cotangent, gate, up, down)


def table_row(table, number):
    table = jnp.asarray(table, jnp.int32)
    row = lax.dynamic_slice(
        table, (number, 0), (1, table.shape[1]), allow_negative_indices=False
    )[0]
    return [row[k] for k in range(table.shape[1])]


class Ring:
    def __init__(self, axis, count):
        self.axis = axis
        self.count = count
        order = [0, 2, 4, 6, 7, 5, 3, 1] if count == 8 else list(range(count))
        place = [order.index(k) for k in range(count)]
        self.members = table_row(
            [[order[(place[k] + hop) % count] for hop in range(count)] for k in range(count)],
            lax.axis_index(axis),
        )
        self.right = [(order[k], order[(k + 1) % count]) for k in range(count)]
        self.left = [(b, a) for a, b in self.right]

    def go_right(self, value):
        return lax.ppermute(value, self.axis, self.right)

    def go_left(self, value):
        return lax.ppermute(value, self.axis, self.left)

    def member(self, offset):
        return self.members[offset % self.count]

    def gather(self, block, axis=0, out_type=None):
        count, rows = self.count, block.shape[axis]
        half = rows // 2
        out_type = out_type or block.dtype
        shape = list(block.shape)
        shape[axis] = count * rows
        out = jnp.zeros(shape, out_type)

        def put(out, value, offset, shift=0):
            start = [0] * block.ndim
            start[axis] = self.member(offset) * rows + shift
            return lax.dynamic_update_slice(
                out, value.astype(out_type), start, allow_negative_indices=False
            )

        right = left = block
        put_next = [(block, 0, 0)]
        for hop in range(1, (count - 1) // 2 + 1):
            right, left = yield right, left
            for item in put_next:
                out = put(out, *item)
            right, left, out = lax.optimization_barrier((right, left, out))
            put_next = [(right, -hop, 0), (left, hop, 0)]
        if count % 2 == 0:
            far = count // 2
            near_half = lax.slice_in_dim(right, 0, half, axis=axis)
            far_half = lax.slice_in_dim(left, half, rows, axis=axis)
            right, left = yield near_half, far_half
            put_next += [(right, -far, 0), (left, far, half)]
        for item in put_next:
            out = put(out, *item)
        return out

    def scatter_sum(self, whole, axis=0):
        rows = whole.shape[axis] // self.count
        half = rows // 2
        shape = list(whole.shape)
        blocks = whole.reshape(shape[:axis] + [self.count, rows] + shape[axis + 1 :])
        sizes = shape[:axis] + [1, half] + shape[axis + 1 :]

        def pick(offset, shift):
            start = [0] * blocks.ndim
            start[axis], start[axis + 1] = self.member(offset), shift
            value = lax.dynamic_slice(blocks, start, sizes, allow_negative_indices=False)
            return jnp.squeeze(value, axis)

        right, left = pick(-1, 0), pick(1, half)
        for hop in range(1, self.count):
            right, left = yield right, left
            right = right.astype(f32) + pick(-1 - hop, 0).astype(f32)
            left = left.astype(f32) + pick(1 + hop, half).astype(f32)
            if hop < self.count - 1:
                right, left = right.astype(bf16), left.astype(bf16)
        return right, left

    def sum_all(self, shard):
        halves = yield from self.scatter_sum(shard)
        block = jnp.concatenate([part.astype(bf16) for part in halves], axis=0)
        return (yield from self.gather(block, out_type=f32))

    def run(self, chains):
        results, arrived, token = {}, {}, None
        number = 0
        while len(results) < len(chains):
            turns = max(hops for start, hops, steps in chains)
            for turn in range(turns):
                for k, (start, hops, steps) in enumerate(chains):
                    if k in results or number < start or turn >= hops:
                        continue
                    try:
                        payload = steps.send(arrived.get(k))
                    except StopIteration as stop:
                        results[k] = stop.value
                        continue
                    if token is not None:
                        payload, token = lax.optimization_barrier((payload, token))
                    token = payload[0]
                    arrived[k] = (self.go_right(payload[0]), self.go_left(payload[1]))
            number += 1
        return [results[k] for k in range(len(chains))]


class Cube:
    def __init__(self, axis, count):
        self.axis = axis
        self.count = count
        self.members = table_row(
            [[k ^ key for key in range(count)] for k in range(count)], lax.axis_index(axis)
        )
        self.bits = [1 << k for k in range(count.bit_length() - 1)]

    def swap(self, value, bit):
        return lax.ppermute(value, self.axis, [(k, k ^ bit) for k in range(self.count)])

    def gather(self, shard):
        held = {0: shard}
        for bit in reversed(self.bits):
            held.update({key ^ bit: self.swap(value, bit) for key, value in held.items()})
        rows = shard.shape[0]
        out = jnp.zeros((self.count * rows,) + shard.shape[1:], shard.dtype)
        for key, value in held.items():
            start = (self.members[key] * rows,) + (0,) * (shard.ndim - 1)
            out = lax.dynamic_update_slice(out, value, start, allow_negative_indices=False)
        return out

    def scatter_sum(self, whole):
        blocks = whole.reshape((self.count, whole.shape[0] // self.count) + whole.shape[1:])
        held = {
            key: lax.dynamic_slice(
                blocks,
                (self.members[key],) + (0,) * whole.ndim,
                (1,) + blocks.shape[1:],
                allow_negative_indices=False,
            )[0]
            for key in range(self.count)
        }
        for bit in self.bits:
            far = [key for key in held if key & bit]
            arrived = yield bit, [held.pop(key) for key in far]
            for key, value in zip(far, arrived):
                kept = key ^ bit
                held[kept] = (held[kept].astype(f32) + value.astype(f32)).astype(bf16)
        return held[0]

    def send(self, payload):
        bit, values = payload
        return [self.swap(value, bit) for value in values]

    def finish(self, steps, arrived=None):
        while True:
            try:
                arrived = self.send(steps.send(arrived))
            except StopIteration as stop:
                return stop.value


def layout(lengths, places):
    ends = jnp.cumsum(lengths)
    starts = ends - lengths
    member = jnp.sum((places[:, None] >= ends[None, :]).astype(jnp.int32), axis=1)
    chosen = member[:, None] == jnp.arange(lengths.shape[0], dtype=jnp.int32)[None, :]
    return jnp.sum(jnp.where(chosen, starts[None, :], 0), axis=1)


def body(
    fsdp_count,
    ctx_count,
    tokens,
    seq_lengths,
    attn_gain,
    w_query,
    w_key,
    w_value,
    query_gain,
    key_gain,
    w_output,
    mlp_gain,
    w_gate,
    w_up,
    w_down,
    out_grad,
):
    groups, rows, width = tokens.shape
    total = rows * ctx_count
    flat_rows = groups * rows
    ctx = lax.axis_index("ctx")
    ring, cube = Ring("ctx", ctx_count), Cube("fsdp", fsdp_count)

    query_heads, key_heads = w_query.shape[1] // HD, w_key.shape[1] // HD
    heads = query_heads // ctx_count
    query_width = heads * HD
    shared = ctx_count // key_heads
    key_head = ctx // shared
    w_mine = jnp.concatenate(
        [
            lax.dynamic_slice(w_query, (0, ctx * query_width), (w_query.shape[0], query_width)),
            lax.dynamic_slice(w_key, (0, key_head * HD), (w_key.shape[0], HD)),
            lax.dynamic_slice(w_value, (0, key_head * HD), (w_value.shape[0], HD)),
        ],
        axis=1,
    )
    packed = jnp.concatenate([attn_gain, mlp_gain, query_gain, key_gain])
    all_gains = cube.gather(packed[None, :]).astype(f32)
    d_shard, h_shard = attn_gain.shape[0], query_gain.shape[0]
    gain_attn = all_gains[:, :d_shard].reshape(-1)
    gain_mlp = all_gains[:, d_shard : 2 * d_shard].reshape(-1)
    gain_query = all_gains[:, 2 * d_shard : 2 * d_shard + h_shard].reshape(-1)
    gain_key = all_gains[:, 2 * d_shard + h_shard :].reshape(-1)
    head_gains = jnp.stack([gain_query, gain_key])
    w_heads = cube.gather(w_mine)

    full_output = lax.all_gather(w_output, "fsdp", axis=0, tiled=True)
    full_gate = lax.all_gather(w_gate, "fsdp", axis=0, tiled=True)
    full_up = lax.all_gather(w_up, "fsdp", axis=0, tiled=True)
    full_down = lax.all_gather(w_down, "fsdp", axis=0, tiled=True)

    places = jnp.arange(total, dtype=jnp.int32)
    first = jax.vmap(lambda lengths: layout(lengths, places))(seq_lengths)
    lane = jnp.arange(HD, dtype=jnp.int32)
    inverse = jnp.exp(
        lax.rem(lane, HD // 2).astype(f32) * (-2.0 * math.log(1000000.0) / HD)
    )
    angles = (places[None, :] - first).astype(f32)[:, :, None] * inverse[None, None, :]
    cosine = jnp.cos(angles)
    sine = jnp.sin(angles) * jnp.where(lane < HD // 2, -1.0, 1.0)

    (all_tokens,) = ring.run([(0, 1, ring.gather(tokens, axis=1))])
    group_normed, group_lin, saved, attended = [], [], [], []
    for g in range(groups):
        values = all_tokens[g].astype(f32)
        normed = (values * inverse_rms(values) * gain_attn).astype(bf16)
        lin = matmul(normed, w_heads)
        qkv, att, att_t, lse = attention_forward(
            lin, cosine[g], sine[g], first[g][None, :], head_gains
        )
        back = lax.all_to_all(
            att.reshape(ctx_count, rows, query_width), "ctx", 0, 0, tiled=True
        )
        attended.append(jnp.swapaxes(back, 0, 1).reshape(rows, ctx_count * query_width))
        group_normed.append(normed)
        group_lin.append(lin)
        saved.append((qkv, att_t, lse))

    attended_low = jnp.concatenate(attended, axis=0)

    inputs = tokens.reshape(flat_rows, width).astype(f32)
    cotangent = out_grad.reshape(flat_rows, width)
    middle = inputs + matmul(attended_low, full_output)
    normed_mlp = (middle * inverse_rms(middle) * gain_mlp).astype(bf16)
    hidden, grad_gate_low, grad_up_low, feed_out, grad_normed_mlp = feed_forward(
        normed_mlp, cotangent, full_gate, full_up, full_down
    )
    grad_middle = cotangent.astype(f32) + rms_backward(middle, gain_mlp, grad_normed_mlp)
    grad_branch = grad_middle.astype(bf16)
    group_grad, part = [], None
    for g in range(groups):
        branch = grad_branch[g * rows : (g + 1) * rows]
        if part is not None:
            branch, part = lax.optimization_barrier((branch, part))
        part = contract_cols(branch, full_output).astype(bf16)
        part = jnp.swapaxes(part.reshape(rows, ctx_count, query_width), 0, 1)
        arrived = lax.all_to_all(part, "ctx", 0, 0, tiled=True)
        group_grad.append(arrived.reshape(total, query_width))
    hidden, attended_low, grad_branch, feed_out, part = lax.optimization_barrier(
        (hidden, attended_low, grad_branch, feed_out, part)
    )
    normed_mlp, grad_gate_low, grad_up_low, group_grad[0] = lax.optimization_barrier(
        (normed_mlp, grad_gate_low, grad_up_low, group_grad[0])
    )
    output = (middle + feed_out).astype(bf16)
    shard_down, shard_output, shard_gate, shard_up = [
        lax.psum_scatter(
            contract_rows(left, right).astype(bf16), "fsdp", scatter_dimension=0, tiled=True
        )
        for left, right in (
            (hidden, cotangent),
            (attended_low, grad_branch),
            (normed_mlp, grad_gate_low),
            (normed_mlp, grad_up_low),
        )
    ]

    grad_heads = jnp.zeros(w_heads.shape, f32)
    grad_query_gain = jnp.zeros((1, HD), f32)
    grad_key_gain = jnp.zeros((1, HD), f32)
    group_low, partials = [], []
    for g in range(groups):
        qkv, att_t, lse = saved[g]
        grad_low, query_part, key_part = attention_backward(
            qkv,
            group_lin[g],
            group_grad[g],
            att_t,
            lse,
            cosine[g],
            sine[g],
            first[g][None, :],
            head_gains,
        )
        grad_query_gain = grad_query_gain + query_part
        grad_key_gain = grad_key_gain + key_part
        group_low.append(grad_low)
        partial = contract_cols(grad_low, w_heads).astype(bf16)
        if g + 1 < groups:
            group_grad[g + 1], partial = lax.optimization_barrier((group_grad[g + 1], partial))
        partials.append(partial)
    for g in range(groups):
        grad_heads = grad_heads + contract_rows(group_normed[g], group_low[g])
    partial = jnp.stack(partials)

    small = jnp.concatenate(
        [grad_query_gain.reshape(fsdp_count, h_shard), grad_key_gain.reshape(fsdp_count, h_shard)],
        axis=1,
    )
    small = jnp.pad(small, ((0, 0), (0, d_shard - 2 * h_shard))).reshape(-1, 1)
    small = jnp.pad(small, ((0, 0), (0, HD - 1)))
    mine = cube.finish(
        cube.scatter_sum(jnp.concatenate([grad_heads, small], axis=1).astype(bf16))
    )
    split = shard_down.shape[0]
    shard_rows = jnp.concatenate([shard_down, shard_output], axis=0)
    shard_pair = jnp.concatenate([shard_gate, shard_up], axis=0)
    halves, summed_rows, summed_pair, gathered = ring.run(
        [
            (0, 1, ring.scatter_sum(partial, axis=1)),
            (0, 2, ring.sum_all(shard_rows)),
            (2, 2, ring.sum_all(shard_pair)),
            (4, 2, ring.gather(mine, out_type=f32)),
        ]
    )
    grad_normed = jnp.concatenate(halves, axis=1).reshape(flat_rows, width)
    token_grad = grad_middle + rms_backward(inputs, gain_attn, grad_normed)
    shard_down, shard_output = summed_rows[:split], summed_rows[split:]
    shard_gate, shard_up = summed_pair[:d_shard], summed_pair[d_shard:]
    gathered = gathered.reshape(ctx_count, d_shard, -1)
    shard_query = jnp.swapaxes(gathered[:, :, :query_width], 0, 1).reshape(d_shard, -1)

    def key_columns(start):
        part = gathered[:, :, start : start + HD].reshape(key_heads, shared, d_shard, HD)
        return jnp.swapaxes(jnp.sum(part, axis=1), 0, 1).reshape(d_shard, -1)

    shard_key = key_columns(query_width)
    shard_value = key_columns(query_width + HD)
    head_sums = jnp.sum(gathered[:, : 2 * h_shard, query_width + 2 * HD], axis=0)
    shard_attn_gain = (
        jnp.sum(shard_query * w_query.astype(f32), axis=1)
        + jnp.sum(shard_key * w_key.astype(f32), axis=1)
        + jnp.sum(shard_value * w_value.astype(f32), axis=1)
    ) / attn_gain.astype(f32)
    shard_mlp_gain = (
        jnp.sum(shard_gate * w_gate.astype(f32), axis=1)
        + jnp.sum(shard_up * w_up.astype(f32), axis=1)
    ) / mlp_gain.astype(f32)
    return (
        output.reshape(groups, rows, width),
        token_grad.reshape(groups, rows, width),
        shard_attn_gain,
        shard_query,
        shard_key,
        shard_value,
        head_sums[:h_shard],
        head_sums[h_shard:],
        shard_output,
        shard_mlp_gain,
        shard_gate,
        shard_up,
        shard_down,
    )


def solution(mesh):
    rows, matrix, vector = P("fsdp", "ctx", None), P("fsdp", None), P("fsdp")
    return jax.shard_map(
        functools.partial(body, mesh.shape["fsdp"], mesh.shape["ctx"]),
        mesh=mesh,
        in_specs=(
            rows,
            matrix,
            vector,
            matrix,
            matrix,
            matrix,
            vector,
            vector,
            matrix,
            vector,
            matrix,
            matrix,
            matrix,
            rows,
        ),
        out_specs=(
            rows,
            rows,
            vector,
            matrix,
            matrix,
            matrix,
            vector,
            vector,
            matrix,
            vector,
            matrix,
            matrix,
            matrix,
        ),
        check_vma=False,
    )
```

```python
import functools
import math

import jax
import jax.numpy as jnp
from jax import lax
from jax.experimental import pallas as pl
from jax.experimental.pallas import tpu as pltpu
from jax.sharding import PartitionSpec as P

HD = 128
EPSILON = 1e-06
SCALE = HD ** (-0.5)
LOG2E = math.log2(math.e)
BLOCK = 512
FEED_BLOCK = 512
VMEM_LIMIT = 48 * 1024 * 1024
bf16 = jnp.bfloat16
f32 = jnp.float32


def matmul(left, right):
    return jnp.dot(left, right, preferred_element_type=f32)


def contract_rows(left, right):
    return lax.dot_general(left, right, (((0,), (0,)), ((), ())), preferred_element_type=f32)


def contract_cols(left, right):
    return lax.dot_general(left, right, (((1,), (1,)), ((), ())), preferred_element_type=f32)


def inverse_rms(values):
    return lax.rsqrt(jnp.mean(values * values, axis=-1, keepdims=True) + EPSILON)


def rms_backward(values, gain, grad):
    inverse = inverse_rms(values)
    scaled = grad * gain
    mean = jnp.mean(scaled * values, axis=-1, keepdims=True)
    return inverse * scaled - values * (inverse * inverse * inverse * mean)


def rope(values, cosine, sine):
    return values * cosine + pltpu.roll(values, HD // 2, 1) * sine


def rope_back(grad, cosine, sine):
    return grad * cosine + pltpu.roll(grad * sine, HD // 2, 1)


def visible(first, row, column, size):
    key_places = row * size + lax.broadcasted_iota(jnp.int32, (size, size), 0)
    shown = key_places >= first
    if row == column:
        places = column * size + lax.broadcasted_iota(jnp.int32, (size, size), 1)
        shown = shown & (key_places <= places)
    return shown


def forward_kernel(
    lin_ref, cos_ref, sin_ref, first_ref, gain_ref, qkv_ref, att_ref, att_t_ref, lse_ref, k_scr, vt_scr
):
    step = pl.program_id(0)
    total = lin_ref.shape[0]
    size = min(BLOCK, total)

    @pl.when(step == 1)
    def store_values():
        values = lin_ref[...]
        qkv_ref[...] = values.astype(bf16)
        vt_scr[...] = values.T.astype(bf16)

    @pl.when(step != 1)
    def store_rotated():
        gain = jnp.where(step == 0, gain_ref[1:2, :], gain_ref[0:1, :])
        linear = lin_ref[...]
        normed = linear * inverse_rms(linear) * gain
        qkv_ref[...] = rope(normed, cos_ref[...], sin_ref[...]).astype(bf16)

    @pl.when(step == 0)
    def keep_keys():
        k_scr[...] = qkv_ref[...]

    @pl.when(step >= 2)
    def attend():
        for i in range(total // size):
            cols = slice(i * size, (i + 1) * size)
            queries = qkv_ref[cols, :]
            first = first_ref[:, cols]
            weight = jnp.zeros((1, size), f32)
            acc = jnp.zeros((HD, size), f32)
            for j in range(i + 1):
                rows = slice(j * size, (j + 1) * size)
                scores = contract_cols(k_scr[rows, :], queries) * (SCALE * LOG2E)
                probs = jnp.where(visible(first, j, i, size), jnp.exp2(scores), 0.0)
                weight = weight + jnp.sum(probs, axis=0, keepdims=True)
                acc = acc + matmul(vt_scr[:, rows], probs.astype(bf16))
            acc = acc * (1.0 / weight)
            att_t_ref[0, :, cols] = acc
            att_ref[cols, :] = acc.T.astype(bf16)
            lse_ref[0, :, cols] = jnp.log2(weight)


def attention_forward(lin, cosine, sine, first, gains):
    total, width = lin.shape
    heads = width // HD - 2
    last = heads + 2

    def column(t):
        return (0, jnp.where(t < 2, heads + t, t - 2))

    def query_column(t):
        return (0, jnp.maximum(t - 2, 0))

    full = lambda shape: pl.BlockSpec(shape, lambda t: (0,) * len(shape))
    return pl.pallas_call(
        forward_kernel,
        grid=(last,),
        out_shape=(
            jax.ShapeDtypeStruct((total, width), bf16),
            jax.ShapeDtypeStruct((total, heads * HD), bf16),
            jax.ShapeDtypeStruct((heads, HD, total), f32),
            jax.ShapeDtypeStruct((heads, 1, total), f32),
        ),
        in_specs=[
            pl.BlockSpec((total, HD), column),
            full((total, HD)),
            full((total, HD)),
            full((1, total)),
            full((2, HD)),
        ],
        out_specs=(
            pl.BlockSpec((total, HD), column),
            pl.BlockSpec((total, HD), query_column),
            pl.BlockSpec((1, HD, total), lambda t: (jnp.maximum(t - 2, 0), 0, 0)),
            pl.BlockSpec((1, 1, total), lambda t: (jnp.maximum(t - 2, 0), 0, 0)),
        ),
        scratch_shapes=[pltpu.VMEM((total, HD), bf16), pltpu.VMEM((HD, total), bf16)],
        compiler_params=pltpu.CompilerParams(vmem_limit_bytes=VMEM_LIMIT),
        cost_estimate=pl.CostEstimate(
            flops=heads * total * total * HD * 4,
            bytes_accessed=total * width * 12,
            transcendentals=heads * total * total // 2,
        ),
        name="attention_forward",
    )(lin, cosine, sine, first, gains)


def backward_kernel(
    q_ref,
    k_ref,
    v_ref,
    lin_ref,
    do_ref,
    att_t_ref,
    lse_ref,
    cos_ref,
    sin_ref,
    first_ref,
    gain_ref,
    out_ref,
    q_gain_ref,
    k_gain_ref,
    kt_scr,
    dk_scr,
    dv_scr,
):
    step = pl.program_id(0)
    heads = pl.num_programs(0) - 2
    total = q_ref.shape[0]
    size = min(BLOCK, total)

    @pl.when(step == 0)
    def clear():
        kt_scr[...] = k_ref[...].astype(f32).T.astype(bf16)
        dk_scr[...] = jnp.zeros_like(dk_scr)
        dv_scr[...] = jnp.zeros_like(dv_scr)
        q_gain_ref[...] = jnp.zeros_like(q_gain_ref)

    def norm_back(grad, rows, gain):
        turned = rope_back(grad, cos_ref[rows, :], sin_ref[rows, :])
        linear = lin_ref[rows, :]
        inverse = inverse_rms(linear)
        gain_part = jnp.sum(turned * (linear * inverse), axis=0, keepdims=True)
        scaled = turned * gain
        mean = jnp.mean(scaled * linear, axis=-1, keepdims=True)
        out_ref[rows, :] = (
            inverse * scaled - linear * (inverse * inverse * inverse * mean)
        ).astype(bf16)
        return gain_part

    @pl.when(step < heads)
    def head():
        for i in range(total // size):
            cols = slice(i * size, (i + 1) * size)
            queries = q_ref[cols, :]
            grads = do_ref[cols, :]
            delta = jnp.sum(grads.astype(f32).T * att_t_ref[0, :, cols], axis=0, keepdims=True)
            first = first_ref[:, cols]
            lse = lse_ref[0, :, cols]
            acc = jnp.zeros((HD, size), f32)
            for j in range(i + 1):
                rows = slice(j * size, (j + 1) * size)
                scores = contract_cols(k_ref[rows, :], queries) * (SCALE * LOG2E)
                probs = jnp.where(visible(first, j, i, size), jnp.exp2(scores - lse), 0.0)
                grad_probs = contract_cols(v_ref[rows, :], grads)
                grad_scores = (probs * (grad_probs - delta)).astype(bf16)
                dv_scr[rows, :] += matmul(probs.astype(bf16), grads)
                dk_scr[rows, :] += matmul(grad_scores, queries)
                acc = acc + matmul(kt_scr[:, rows], grad_scores)
            q_gain_ref[...] += norm_back((acc * SCALE).T, cols, gain_ref[0:1, :])

    @pl.when(step == heads)
    def keys():
        part = jnp.zeros((1, HD), f32)
        for i in range(total // size):
            rows = slice(i * size, (i + 1) * size)
            part = part + norm_back(dk_scr[rows, :] * SCALE, rows, gain_ref[1:2, :])
        k_gain_ref[...] = part

    @pl.when(step == heads + 1)
    def values():
        out_ref[...] = dv_scr[...].astype(bf16)


def attention_backward(qkv, lin, grad, att_t, lse, cosine, sine, first, gains):
    total, width = lin.shape
    heads = width // HD - 2
    last = heads + 2

    def query_column(t):
        return (0, jnp.minimum(t, heads - 1))

    full = lambda shape: pl.BlockSpec(shape, lambda t: (0,) * len(shape))
    return pl.pallas_call(
        backward_kernel,
        grid=(last,),
        out_shape=(
            jax.ShapeDtypeStruct((total, width), bf16),
            jax.ShapeDtypeStruct((1, HD), f32),
            jax.ShapeDtypeStruct((1, HD), f32),
        ),
        in_specs=[
            pl.BlockSpec((total, HD), query_column),
            pl.BlockSpec((total, HD), lambda t: (0, heads)),
            pl.BlockSpec((total, HD), lambda t: (0, heads + 1)),
            pl.BlockSpec((total, HD), lambda t: (0, jnp.minimum(t, heads))),
            pl.BlockSpec((total, HD), query_column),
            pl.BlockSpec((1, HD, total), lambda t: (jnp.minimum(t, heads - 1), 0, 0)),
            pl.BlockSpec((1, 1, total), lambda t: (jnp.minimum(t, heads - 1), 0, 0)),
            full((total, HD)),
            full((total, HD)),
            full((1, total)),
            full((2, HD)),
        ],
        out_specs=(
            pl.BlockSpec((total, HD), lambda t: (0, t)),
            full((1, HD)),
            full((1, HD)),
        ),
        scratch_shapes=[
            pltpu.VMEM((HD, total), bf16),
            pltpu.VMEM((total, HD), f32),
            pltpu.VMEM((total, HD), f32),
        ],
        compiler_params=pltpu.CompilerParams(vmem_limit_bytes=VMEM_LIMIT),
        cost_estimate=pl.CostEstimate(
            flops=heads * total * total * HD * 10,
            bytes_accessed=total * width * 12,
            transcendentals=heads * total * total // 2,
        ),
        name="attention_backward",
    )(qkv, qkv, qkv, lin, grad, att_t, lse, cosine, sine, first, gains)


def feed_kernel(*refs):
    x_ref, cot_ref, gate_ref, up_ref, down_ref = refs[:5]
    hid_ref, grad_gate_ref, grad_up_ref, out_ref, back_ref = refs[-5:]
    step = pl.program_id(0)
    total = x_ref.shape[0]
    size = min(128, total)

    @pl.when(step == 0)
    def clear():
        out_ref[...] = jnp.zeros_like(out_ref)
        back_ref[...] = jnp.zeros_like(back_ref)

    for i in range(total // size):
        rows = slice(i * size, (i + 1) * size)
        gate = matmul(x_ref[rows, :], gate_ref[...])
        upward = matmul(x_ref[rows, :], up_ref[...])
        grad_hidden = contract_cols(cot_ref[rows, :], down_ref[...])
        sigmoid = 1.0 / (1.0 + jnp.exp(-gate))
        activated = gate * sigmoid
        hidden = (activated * upward).astype(bf16)
        hid_ref[rows, :] = hidden
        slope = sigmoid * (1.0 + gate * (1.0 - sigmoid))
        grad_gate = (grad_hidden * upward * slope).astype(bf16)
        grad_up = (grad_hidden * activated).astype(bf16)
        grad_gate_ref[rows, :] = grad_gate
        grad_up_ref[rows, :] = grad_up
        out_ref[rows, :] += matmul(hidden, down_ref[...])
        back_ref[rows, :] += contract_cols(grad_gate, gate_ref[...]) + contract_cols(
            grad_up, up_ref[...]
        )


def feed_forward(group, groups, earlier, normed, cotangent, gate, up, down):
    total, width = normed.shape
    hidden_width = down.shape[0]
    block = min(FEED_BLOCK, hidden_width)
    whole = pl.BlockSpec((total, width), lambda t: (0, 0))
    placed = pl.BlockSpec((total, block), lambda t: (group, t))
    kept = jax.ShapeDtypeStruct((groups * total, hidden_width), bf16)
    return pl.pallas_call(
        feed_kernel,
        grid=(hidden_width // block,),
        out_shape=(
            kept,
            kept,
            kept,
            jax.ShapeDtypeStruct((total, width), f32),
            jax.ShapeDtypeStruct((total, width), f32),
        ),
        in_specs=[
            whole,
            whole,
            pl.BlockSpec((width, block), lambda t: (0, t)),
            pl.BlockSpec((width, block), lambda t: (0, t)),
            pl.BlockSpec((block, width), lambda t: (t, 0)),
        ]
        + [pl.BlockSpec(memory_space=pl.ANY)] * len(earlier),
        out_specs=(placed, placed, placed, whole, whole),
        input_output_aliases={5 + k: k for k in range(len(earlier))},
        compiler_params=pltpu.CompilerParams(vmem_limit_bytes=VMEM_LIMIT),
        cost_estimate=pl.CostEstimate(
            flops=total * width * hidden_width * 12,
            bytes_accessed=hidden_width * (6 * width + 6 * total) + total * width * 12,
            transcendentals=total * hidden_width,
        ),
        name="feed_forward",
    )(normed, cotangent, gate, up, down, *earlier)


def table_row(table, number):
    table = jnp.asarray(table, jnp.int32)
    row = lax.dynamic_slice(
        table, (number, 0), (1, table.shape[1]), allow_negative_indices=False
    )[0]
    return [row[k] for k in range(table.shape[1])]


class Ring:
    def __init__(self, axis, count):
        self.axis = axis
        self.count = count
        order = [0, 2, 4, 6, 7, 5, 3, 1] if count == 8 else list(range(count))
        place = [order.index(k) for k in range(count)]
        self.members = table_row(
            [[order[(place[k] + hop) % count] for hop in range(count)] for k in range(count)],
            lax.axis_index(axis),
        )
        self.right = [(order[k], order[(k + 1) % count]) for k in range(count)]
        self.left = [(b, a) for a, b in self.right]

    def go_right(self, value):
        return lax.ppermute(value, self.axis, self.right)

    def go_left(self, value):
        return lax.ppermute(value, self.axis, self.left)

    def member(self, offset):
        return self.members[offset % self.count]

    def gather(self, block, axis=0, out_type=None):
        count, rows = self.count, block.shape[axis]
        half = rows // 2
        out_type = out_type or block.dtype
        shape = list(block.shape)
        shape[axis] = count * rows
        out = jnp.zeros(shape, out_type)

        def put(out, value, offset, shift=0):
            start = [0] * block.ndim
            start[axis] = self.member(offset) * rows + shift
            return lax.dynamic_update_slice(
                out, value.astype(out_type), start, allow_negative_indices=False
            )

        right = left = block
        put_next = [(block, 0, 0)]
        for hop in range(1, (count - 1) // 2 + 1):
            right, left = yield right, left
            for item in put_next:
                out = put(out, *item)
            right, left, out = lax.optimization_barrier((right, left, out))
            put_next = [(right, -hop, 0), (left, hop, 0)]
        if count % 2 == 0:
            far = count // 2
            near_half = lax.slice_in_dim(right, 0, half, axis=axis)
            far_half = lax.slice_in_dim(left, half, rows, axis=axis)
            right, left = yield near_half, far_half
            put_next += [(right, -far, 0), (left, far, half)]
        for item in put_next:
            out = put(out, *item)
        return out

    def scatter_sum(self, parts):
        rows = parts[0].shape[0] // self.count
        half = rows // 2
        blocks = [part.reshape((self.count, rows) + part.shape[1:]) for part in parts]
        sizes = (1, half) + parts[0].shape[1:]

        def pick(offset, shift):
            start = (self.member(offset), shift) + (0,) * (parts[0].ndim - 1)
            values = [
                lax.dynamic_slice(block, start, sizes, allow_negative_indices=False)
                for block in blocks
            ]
            return jnp.concatenate(values, axis=0)

        right, left = pick(-1, 0), pick(1, half)
        for hop in range(1, self.count):
            right, left = yield right, left
            right = right.astype(f32) + pick(-1 - hop, 0).astype(f32)
            left = left.astype(f32) + pick(1 + hop, half).astype(f32)
            if hop < self.count - 1:
                right, left = right.astype(bf16), left.astype(bf16)
        return right, left

    def sum_all(self, shard):
        halves = yield from self.scatter_sum([shard])
        block = jnp.concatenate([part[0].astype(bf16) for part in halves], axis=0)
        return (yield from self.gather(block, out_type=f32))

    def run(self, chains):
        results, arrived, token = {}, {}, None
        number = 0
        while len(results) < len(chains):
            turns = max(hops for start, hops, steps in chains)
            for turn in range(turns):
                for k, (start, hops, steps) in enumerate(chains):
                    if k in results or number < start or turn >= hops:
                        continue
                    try:
                        payload = steps.send(arrived.get(k))
                    except StopIteration as stop:
                        results[k] = stop.value
                        continue
                    if token is not None:
                        payload, token = lax.optimization_barrier((payload, token))
                    token = payload[0]
                    arrived[k] = (self.go_right(payload[0]), self.go_left(payload[1]))
            number += 1
        return [results[k] for k in range(len(chains))]


class Cube:
    def __init__(self, axis, count):
        self.axis = axis
        self.count = count
        self.members = table_row(
            [[k ^ key for key in range(count)] for k in range(count)], lax.axis_index(axis)
        )
        self.bits = [1 << k for k in range(count.bit_length() - 1)]

    def swap(self, value, bit):
        return lax.ppermute(value, self.axis, [(k, k ^ bit) for k in range(self.count)])

    def gather(self, shard):
        held = {0: shard}
        for bit in reversed(self.bits):
            held.update({key ^ bit: self.swap(value, bit) for key, value in held.items()})
        rows = shard.shape[0]
        out = jnp.zeros((self.count * rows,) + shard.shape[1:], shard.dtype)
        for key, value in held.items():
            start = (self.members[key] * rows,) + (0,) * (shard.ndim - 1)
            out = lax.dynamic_update_slice(out, value, start, allow_negative_indices=False)
        return out

    def scatter_sum(self, whole):
        blocks = whole.reshape((self.count, whole.shape[0] // self.count) + whole.shape[1:])
        held = {
            key: lax.dynamic_slice(
                blocks,
                (self.members[key],) + (0,) * whole.ndim,
                (1,) + blocks.shape[1:],
                allow_negative_indices=False,
            )[0]
            for key in range(self.count)
        }
        for bit in self.bits:
            far = [key for key in held if key & bit]
            arrived = yield bit, [held.pop(key) for key in far]
            for key, value in zip(far, arrived):
                kept = key ^ bit
                held[kept] = (held[kept].astype(f32) + value.astype(f32)).astype(bf16)
        return held[0]

    def send(self, payload):
        bit, values = payload
        return [self.swap(value, bit) for value in values]

    def finish(self, steps, arrived=None):
        while True:
            try:
                arrived = self.send(steps.send(arrived))
            except StopIteration as stop:
                return stop.value


def layout(lengths, places):
    ends = jnp.cumsum(lengths)
    starts = ends - lengths
    member = jnp.sum((places[:, None] >= ends[None, :]).astype(jnp.int32), axis=1)
    chosen = member[:, None] == jnp.arange(lengths.shape[0], dtype=jnp.int32)[None, :]
    return jnp.sum(jnp.where(chosen, starts[None, :], 0), axis=1)


def body(
    fsdp_count,
    ctx_count,
    tokens,
    seq_lengths,
    attn_gain,
    w_query,
    w_key,
    w_value,
    query_gain,
    key_gain,
    w_output,
    mlp_gain,
    w_gate,
    w_up,
    w_down,
    out_grad,
):
    groups, rows, width = tokens.shape
    total = rows * ctx_count
    flat_rows = groups * rows
    ctx = lax.axis_index("ctx")
    ring, cube = Ring("ctx", ctx_count), Cube("fsdp", fsdp_count)

    query_heads, key_heads = w_query.shape[1] // HD, w_key.shape[1] // HD
    heads = query_heads // ctx_count
    query_width = heads * HD
    shared = ctx_count // key_heads
    key_head = ctx // shared
    w_mine = jnp.concatenate(
        [
            lax.dynamic_slice(w_query, (0, ctx * query_width), (w_query.shape[0], query_width)),
            lax.dynamic_slice(w_key, (0, key_head * HD), (w_key.shape[0], HD)),
            lax.dynamic_slice(w_value, (0, key_head * HD), (w_value.shape[0], HD)),
        ],
        axis=1,
    )
    packed = jnp.concatenate([attn_gain, mlp_gain, query_gain, key_gain])
    all_gains = cube.gather(packed[None, :]).astype(f32)
    d_shard, h_shard = attn_gain.shape[0], query_gain.shape[0]
    gain_attn = all_gains[:, :d_shard].reshape(-1)
    gain_mlp = all_gains[:, d_shard : 2 * d_shard].reshape(-1)
    gain_query = all_gains[:, 2 * d_shard : 2 * d_shard + h_shard].reshape(-1)
    gain_key = all_gains[:, 2 * d_shard + h_shard :].reshape(-1)
    head_gains = jnp.stack([gain_query, gain_key])
    w_heads = cube.gather(w_mine)

    full_output = lax.all_gather(w_output, "fsdp", axis=0, tiled=True)
    full_gate = lax.all_gather(w_gate, "fsdp", axis=0, tiled=True)
    full_up = lax.all_gather(w_up, "fsdp", axis=0, tiled=True)
    full_down = lax.all_gather(w_down, "fsdp", axis=0, tiled=True)

    places = jnp.arange(total, dtype=jnp.int32)
    first = jax.vmap(lambda lengths: layout(lengths, places))(seq_lengths)
    lane = jnp.arange(HD, dtype=jnp.int32)
    inverse = jnp.exp(
        lax.rem(lane, HD // 2).astype(f32) * (-2.0 * math.log(1000000.0) / HD)
    )
    angles = (places[None, :] - first).astype(f32)[:, :, None] * inverse[None, None, :]
    cosine = jnp.cos(angles)
    sine = jnp.sin(angles) * jnp.where(lane < HD // 2, -1.0, 1.0)

    (all_tokens,) = ring.run([(0, 1, ring.gather(tokens, axis=1))])
    group_normed, group_lin, saved, attended = [], [], [], []
    for g in range(groups):
        values = all_tokens[g].astype(f32)
        normed = (values * inverse_rms(values) * gain_attn).astype(bf16)
        lin = matmul(normed, w_heads)
        qkv, att, att_t, lse = attention_forward(
            lin, cosine[g], sine[g], first[g][None, :], head_gains
        )
        back = lax.all_to_all(
            att.reshape(ctx_count, rows, query_width), "ctx", 0, 0, tiled=True
        )
        attended.append(jnp.swapaxes(back, 0, 1).reshape(rows, ctx_count * query_width))
        group_normed.append(normed)
        group_lin.append(lin)
        saved.append((qkv, att_t, lse))

    inputs = tokens.reshape(flat_rows, width).astype(f32)
    cotangent = out_grad.reshape(flat_rows, width)
    earlier, tag = (), att
    group_grad, kept = [], []
    for g in range(groups):
        attended[g], tag = lax.optimization_barrier((attended[g], tag))
        middle = tokens[g].astype(f32) + matmul(attended[g], full_output)
        normed = (middle * inverse_rms(middle) * gain_mlp).astype(bf16)
        *earlier, feed_out, grad_normed = feed_forward(
            g, groups, earlier, normed, out_grad[g], full_gate, full_up, full_down
        )
        grad = out_grad[g].astype(f32) + rms_backward(middle, gain_mlp, grad_normed)
        branch = grad.astype(bf16)
        part = contract_cols(branch, full_output).astype(bf16)
        part = jnp.swapaxes(part.reshape(rows, ctx_count, query_width), 0, 1)
        arrived = lax.all_to_all(part, "ctx", 0, 0, tiled=True)
        group_grad.append(arrived.reshape(total, query_width))
        kept.append((normed, grad, branch, (middle + feed_out).astype(bf16), attended[g]))
        tag = part
    kept, earlier, tag = lax.optimization_barrier((kept, tuple(earlier), tag))
    hidden, grad_gate_low, grad_up_low = earlier
    normed_mlp, grad_middle, grad_branch, output, attended_low = [
        jnp.concatenate(values, axis=0) for values in zip(*kept)
    ]
    shard_down, shard_output, shard_gate, shard_up = [
        lax.psum_scatter(
            contract_rows(left, right).astype(bf16), "fsdp", scatter_dimension=0, tiled=True
        )
        for left, right in (
            (hidden, cotangent),
            (attended_low, grad_branch),
            (normed_mlp, grad_gate_low),
            (normed_mlp, grad_up_low),
        )
    ]

    grad_heads = jnp.zeros(w_heads.shape, f32)
    grad_query_gain = jnp.zeros((1, HD), f32)
    grad_key_gain = jnp.zeros((1, HD), f32)
    group_low, partials = [], []
    for g in range(groups):
        qkv, att_t, lse = saved[g]
        grad_low, query_part, key_part = attention_backward(
            qkv,
            group_lin[g],
            group_grad[g],
            att_t,
            lse,
            cosine[g],
            sine[g],
            first[g][None, :],
            head_gains,
        )
        grad_query_gain = grad_query_gain + query_part
        grad_key_gain = grad_key_gain + key_part
        group_low.append(grad_low)
        partial = contract_cols(grad_low, w_heads).astype(bf16)
        if g + 1 < groups:
            group_grad[g + 1], partial = lax.optimization_barrier((group_grad[g + 1], partial))
        partials.append(partial)
    for g in range(groups):
        grad_heads = grad_heads + contract_rows(group_normed[g], group_low[g])

    small = jnp.concatenate(
        [grad_query_gain.reshape(fsdp_count, h_shard), grad_key_gain.reshape(fsdp_count, h_shard)],
        axis=1,
    )
    small = jnp.pad(small, ((0, 0), (0, d_shard - 2 * h_shard))).reshape(-1, 1)
    small = jnp.pad(small, ((0, 0), (0, HD - 1)))
    mine = cube.finish(
        cube.scatter_sum(jnp.concatenate([grad_heads, small], axis=1).astype(bf16))
    )
    split = shard_down.shape[0]
    shard_rows = jnp.concatenate([shard_down, shard_output], axis=0)
    shard_pair = jnp.concatenate([shard_gate, shard_up], axis=0)
    halves, summed_rows, summed_pair, gathered = ring.run(
        [
            (0, 1, ring.scatter_sum(partials)),
            (0, 2, ring.sum_all(shard_rows)),
            (3, 2, ring.sum_all(shard_pair)),
            (4, 2, ring.gather(mine, out_type=f32)),
        ]
    )
    grad_normed = jnp.concatenate(halves, axis=1).reshape(flat_rows, width)
    token_grad = grad_middle + rms_backward(inputs, gain_attn, grad_normed)
    shard_down, shard_output = summed_rows[:split], summed_rows[split:]
    shard_gate, shard_up = summed_pair[:d_shard], summed_pair[d_shard:]
    gathered = gathered.reshape(ctx_count, d_shard, -1)
    shard_query = jnp.swapaxes(gathered[:, :, :query_width], 0, 1).reshape(d_shard, -1)

    def key_columns(start):
        part = gathered[:, :, start : start + HD].reshape(key_heads, shared, d_shard, HD)
        return jnp.swapaxes(jnp.sum(part, axis=1), 0, 1).reshape(d_shard, -1)

    shard_key = key_columns(query_width)
    shard_value = key_columns(query_width + HD)
    head_sums = jnp.sum(gathered[:, : 2 * h_shard, query_width + 2 * HD], axis=0)
    shard_attn_gain = (
        jnp.sum(shard_query * w_query.astype(f32), axis=1)
        + jnp.sum(shard_key * w_key.astype(f32), axis=1)
        + jnp.sum(shard_value * w_value.astype(f32), axis=1)
    ) / attn_gain.astype(f32)
    shard_mlp_gain = (
        jnp.sum(shard_gate * w_gate.astype(f32), axis=1)
        + jnp.sum(shard_up * w_up.astype(f32), axis=1)
    ) / mlp_gain.astype(f32)
    return (
        output.reshape(groups, rows, width),
        token_grad.reshape(groups, rows, width),
        shard_attn_gain,
        shard_query,
        shard_key,
        shard_value,
        head_sums[:h_shard],
        head_sums[h_shard:],
        shard_output,
        shard_mlp_gain,
        shard_gate,
        shard_up,
        shard_down,
    )


def solution(mesh):
    rows, matrix, vector = P("fsdp", "ctx", None), P("fsdp", None), P("fsdp")
    return jax.shard_map(
        functools.partial(body, mesh.shape["fsdp"], mesh.shape["ctx"]),
        mesh=mesh,
        in_specs=(
            rows,
            matrix,
            vector,
            matrix,
            matrix,
            matrix,
            vector,
            vector,
            matrix,
            vector,
            matrix,
            matrix,
            matrix,
            rows,
        ),
        out_specs=(
            rows,
            rows,
            vector,
            matrix,
            matrix,
            matrix,
            vector,
            vector,
            matrix,
            vector,
            matrix,
            matrix,
            matrix,
        ),
        check_vma=False,
    )
```

```python
import functools
import math

import jax
import jax.numpy as jnp
from jax import lax
from jax.experimental import pallas as pl
from jax.experimental.pallas import tpu as pltpu
from jax.sharding import PartitionSpec as P

HD = 128
EPSILON = 1e-06
SCALE = HD ** (-0.5)
LOG2E = math.log2(math.e)
BLOCK = 512
FEED_BLOCK = 512
VMEM_LIMIT = 48 * 1024 * 1024
bf16 = jnp.bfloat16
f32 = jnp.float32


def matmul(left, right):
    return jnp.dot(left, right, preferred_element_type=f32)


def contract_rows(left, right):
    return lax.dot_general(left, right, (((0,), (0,)), ((), ())), preferred_element_type=f32)


def contract_cols(left, right):
    return lax.dot_general(left, right, (((1,), (1,)), ((), ())), preferred_element_type=f32)


def inverse_rms(values):
    return lax.rsqrt(jnp.mean(values * values, axis=-1, keepdims=True) + EPSILON)


def rms_backward(values, gain, grad):
    inverse = inverse_rms(values)
    scaled = grad * gain
    mean = jnp.mean(scaled * values, axis=-1, keepdims=True)
    return inverse * scaled - values * (inverse * inverse * inverse * mean)


def rope(values, cosine, sine):
    return values * cosine + pltpu.roll(values, HD // 2, 1) * sine


def rope_back(grad, cosine, sine):
    return grad * cosine + pltpu.roll(grad * sine, HD // 2, 1)


def visible(first, row, column, size):
    key_places = row * size + lax.broadcasted_iota(jnp.int32, (size, size), 0)
    shown = key_places >= first
    if row == column:
        places = column * size + lax.broadcasted_iota(jnp.int32, (size, size), 1)
        shown = shown & (key_places <= places)
    return shown


def forward_kernel(
    lin_ref, cos_ref, sin_ref, first_ref, gain_ref, qkv_ref, att_ref, att_t_ref, lse_ref, k_scr, vt_scr
):
    step = pl.program_id(0)
    total = lin_ref.shape[0]
    size = min(BLOCK, total)

    @pl.when(step == 1)
    def store_values():
        values = lin_ref[...]
        qkv_ref[...] = values.astype(bf16)
        vt_scr[...] = values.T.astype(bf16)

    @pl.when(step != 1)
    def store_rotated():
        gain = jnp.where(step == 0, gain_ref[1:2, :], gain_ref[0:1, :])
        linear = lin_ref[...]
        normed = linear * inverse_rms(linear) * gain
        qkv_ref[...] = rope(normed, cos_ref[...], sin_ref[...]).astype(bf16)

    @pl.when(step == 0)
    def keep_keys():
        k_scr[...] = qkv_ref[...]

    @pl.when(step >= 2)
    def attend():
        for i in range(total // size):
            cols = slice(i * size, (i + 1) * size)
            queries = qkv_ref[cols, :]
            first = first_ref[:, cols]
            weight = jnp.zeros((1, size), f32)
            acc = jnp.zeros((HD, size), f32)
            for j in range(i + 1):
                rows = slice(j * size, (j + 1) * size)
                scores = contract_cols(k_scr[rows, :], queries) * (SCALE * LOG2E)
                probs = jnp.where(visible(first, j, i, size), jnp.exp2(scores), 0.0)
                weight = weight + jnp.sum(probs, axis=0, keepdims=True)
                acc = acc + matmul(vt_scr[:, rows], probs.astype(bf16))
            acc = acc * (1.0 / weight)
            att_t_ref[0, :, cols] = acc
            att_ref[cols, :] = acc.T.astype(bf16)
            lse_ref[0, :, cols] = jnp.log2(weight)


def attention_forward(lin, cosine, sine, first, gains):
    total, width = lin.shape
    heads = width // HD - 2
    last = heads + 2

    def column(t):
        return (0, jnp.where(t < 2, heads + t, t - 2))

    def query_column(t):
        return (0, jnp.maximum(t - 2, 0))

    full = lambda shape: pl.BlockSpec(shape, lambda t: (0,) * len(shape))
    return pl.pallas_call(
        forward_kernel,
        grid=(last,),
        out_shape=(
            jax.ShapeDtypeStruct((total, width), bf16),
            jax.ShapeDtypeStruct((total, heads * HD), bf16),
            jax.ShapeDtypeStruct((heads, HD, total), f32),
            jax.ShapeDtypeStruct((heads, 1, total), f32),
        ),
        in_specs=[
            pl.BlockSpec((total, HD), column),
            full((total, HD)),
            full((total, HD)),
            full((1, total)),
            full((2, HD)),
        ],
        out_specs=(
            pl.BlockSpec((total, HD), column),
            pl.BlockSpec((total, HD), query_column),
            pl.BlockSpec((1, HD, total), lambda t: (jnp.maximum(t - 2, 0), 0, 0)),
            pl.BlockSpec((1, 1, total), lambda t: (jnp.maximum(t - 2, 0), 0, 0)),
        ),
        scratch_shapes=[pltpu.VMEM((total, HD), bf16), pltpu.VMEM((HD, total), bf16)],
        compiler_params=pltpu.CompilerParams(vmem_limit_bytes=VMEM_LIMIT),
        cost_estimate=pl.CostEstimate(
            flops=heads * total * total * HD * 4,
            bytes_accessed=total * width * 12,
            transcendentals=heads * total * total // 2,
        ),
        name="attention_forward",
    )(lin, cosine, sine, first, gains)


def backward_kernel(
    q_ref,
    k_ref,
    v_ref,
    lin_ref,
    do_ref,
    att_t_ref,
    lse_ref,
    cos_ref,
    sin_ref,
    first_ref,
    gain_ref,
    out_ref,
    q_gain_ref,
    k_gain_ref,
    kt_scr,
    dk_scr,
    dv_scr,
):
    step = pl.program_id(0)
    heads = pl.num_programs(0) - 2
    total = q_ref.shape[0]
    size = min(BLOCK, total)

    @pl.when(step == 0)
    def clear():
        kt_scr[...] = k_ref[...].astype(f32).T.astype(bf16)
        dk_scr[...] = jnp.zeros_like(dk_scr)
        dv_scr[...] = jnp.zeros_like(dv_scr)
        q_gain_ref[...] = jnp.zeros_like(q_gain_ref)

    def norm_back(grad, rows, gain):
        turned = rope_back(grad, cos_ref[rows, :], sin_ref[rows, :])
        linear = lin_ref[rows, :]
        inverse = inverse_rms(linear)
        gain_part = jnp.sum(turned * (linear * inverse), axis=0, keepdims=True)
        scaled = turned * gain
        mean = jnp.mean(scaled * linear, axis=-1, keepdims=True)
        out_ref[rows, :] = (
            inverse * scaled - linear * (inverse * inverse * inverse * mean)
        ).astype(bf16)
        return gain_part

    @pl.when(step < heads)
    def head():
        for i in range(total // size):
            cols = slice(i * size, (i + 1) * size)
            queries = q_ref[cols, :]
            grads = do_ref[cols, :]
            delta = jnp.sum(grads.astype(f32).T * att_t_ref[0, :, cols], axis=0, keepdims=True)
            first = first_ref[:, cols]
            lse = lse_ref[0, :, cols]
            acc = jnp.zeros((HD, size), f32)
            for j in range(i + 1):
                rows = slice(j * size, (j + 1) * size)
                scores = contract_cols(k_ref[rows, :], queries) * (SCALE * LOG2E)
                probs = jnp.where(visible(first, j, i, size), jnp.exp2(scores - lse), 0.0)
                grad_probs = contract_cols(v_ref[rows, :], grads)
                grad_scores = (probs * (grad_probs - delta)).astype(bf16)
                dv_scr[rows, :] += matmul(probs.astype(bf16), grads)
                dk_scr[rows, :] += matmul(grad_scores, queries)
                acc = acc + matmul(kt_scr[:, rows], grad_scores)
            q_gain_ref[...] += norm_back((acc * SCALE).T, cols, gain_ref[0:1, :])

    @pl.when(step == heads)
    def keys():
        part = jnp.zeros((1, HD), f32)
        for i in range(total // size):
            rows = slice(i * size, (i + 1) * size)
            part = part + norm_back(dk_scr[rows, :] * SCALE, rows, gain_ref[1:2, :])
        k_gain_ref[...] = part

    @pl.when(step == heads + 1)
    def values():
        out_ref[...] = dv_scr[...].astype(bf16)


def attention_backward(qkv, lin, grad, att_t, lse, cosine, sine, first, gains):
    total, width = lin.shape
    heads = width // HD - 2
    last = heads + 2

    def query_column(t):
        return (0, jnp.minimum(t, heads - 1))

    full = lambda shape: pl.BlockSpec(shape, lambda t: (0,) * len(shape))
    return pl.pallas_call(
        backward_kernel,
        grid=(last,),
        out_shape=(
            jax.ShapeDtypeStruct((total, width), bf16),
            jax.ShapeDtypeStruct((1, HD), f32),
            jax.ShapeDtypeStruct((1, HD), f32),
        ),
        in_specs=[
            pl.BlockSpec((total, HD), query_column),
            pl.BlockSpec((total, HD), lambda t: (0, heads)),
            pl.BlockSpec((total, HD), lambda t: (0, heads + 1)),
            pl.BlockSpec((total, HD), lambda t: (0, jnp.minimum(t, heads))),
            pl.BlockSpec((total, HD), query_column),
            pl.BlockSpec((1, HD, total), lambda t: (jnp.minimum(t, heads - 1), 0, 0)),
            pl.BlockSpec((1, 1, total), lambda t: (jnp.minimum(t, heads - 1), 0, 0)),
            full((total, HD)),
            full((total, HD)),
            full((1, total)),
            full((2, HD)),
        ],
        out_specs=(
            pl.BlockSpec((total, HD), lambda t: (0, t)),
            full((1, HD)),
            full((1, HD)),
        ),
        scratch_shapes=[
            pltpu.VMEM((HD, total), bf16),
            pltpu.VMEM((total, HD), f32),
            pltpu.VMEM((total, HD), f32),
        ],
        compiler_params=pltpu.CompilerParams(vmem_limit_bytes=VMEM_LIMIT),
        cost_estimate=pl.CostEstimate(
            flops=heads * total * total * HD * 10,
            bytes_accessed=total * width * 12,
            transcendentals=heads * total * total // 2,
        ),
        name="attention_backward",
    )(qkv, qkv, qkv, lin, grad, att_t, lse, cosine, sine, first, gains)


def feed_kernel(*refs):
    x_ref, cot_ref, gate_ref, up_ref, down_ref = refs[:5]
    hid_ref, grad_gate_ref, grad_up_ref, out_ref, back_ref = refs[-5:]
    step = pl.program_id(0)
    total = x_ref.shape[0]
    size = 256 if total % 256 == 0 else 128

    @pl.when(step == 0)
    def clear():
        out_ref[...] = jnp.zeros_like(out_ref)
        back_ref[...] = jnp.zeros_like(back_ref)

    for i in range(total // size):
        rows = slice(i * size, (i + 1) * size)
        gate = matmul(x_ref[rows, :], gate_ref[...])
        upward = matmul(x_ref[rows, :], up_ref[...])
        grad_hidden = contract_cols(cot_ref[rows, :], down_ref[...])
        sigmoid = 1.0 / (1.0 + jnp.exp(-gate))
        activated = gate * sigmoid
        hidden = (activated * upward).astype(bf16)
        hid_ref[rows, :] = hidden
        slope = sigmoid * (1.0 + gate * (1.0 - sigmoid))
        grad_gate = (grad_hidden * upward * slope).astype(bf16)
        grad_up = (grad_hidden * activated).astype(bf16)
        grad_gate_ref[rows, :] = grad_gate
        grad_up_ref[rows, :] = grad_up
        out_ref[rows, :] += matmul(hidden, down_ref[...])
        back_ref[rows, :] += contract_cols(grad_gate, gate_ref[...]) + contract_cols(
            grad_up, up_ref[...]
        )


def feed_forward(group, groups, earlier, normed, cotangent, gate, up, down):
    total, width = normed.shape
    hidden_width = down.shape[0]
    block = min(FEED_BLOCK, hidden_width)
    whole = pl.BlockSpec((total, width), lambda t: (0, 0))
    placed = pl.BlockSpec((total, block), lambda t: (group, t))
    kept = jax.ShapeDtypeStruct((groups * total, hidden_width), bf16)
    return pl.pallas_call(
        feed_kernel,
        grid=(hidden_width // block,),
        out_shape=(
            kept,
            kept,
            kept,
            jax.ShapeDtypeStruct((total, width), f32),
            jax.ShapeDtypeStruct((total, width), f32),
        ),
        in_specs=[
            whole,
            whole,
            pl.BlockSpec((width, block), lambda t: (0, t)),
            pl.BlockSpec((width, block), lambda t: (0, t)),
            pl.BlockSpec((block, width), lambda t: (t, 0)),
        ]
        + [pl.BlockSpec(memory_space=pl.ANY)] * len(earlier),
        out_specs=(placed, placed, placed, whole, whole),
        input_output_aliases={5 + k: k for k in range(len(earlier))},
        compiler_params=pltpu.CompilerParams(vmem_limit_bytes=VMEM_LIMIT),
        cost_estimate=pl.CostEstimate(
            flops=total * width * hidden_width * 12,
            bytes_accessed=hidden_width * (6 * width + 6 * total) + total * width * 12,
            transcendentals=total * hidden_width,
        ),
        name="feed_forward",
    )(normed, cotangent, gate, up, down, *earlier)


def table_row(table, number):
    table = jnp.asarray(table, jnp.int32)
    row = lax.dynamic_slice(
        table, (number, 0), (1, table.shape[1]), allow_negative_indices=False
    )[0]
    return [row[k] for k in range(table.shape[1])]


class Ring:
    def __init__(self, axis, count):
        self.axis = axis
        self.count = count
        order = [0, 2, 4, 6, 7, 5, 3, 1] if count == 8 else list(range(count))
        place = [order.index(k) for k in range(count)]
        self.members = table_row(
            [[order[(place[k] + hop) % count] for hop in range(count)] for k in range(count)],
            lax.axis_index(axis),
        )
        self.right = [(order[k], order[(k + 1) % count]) for k in range(count)]
        self.left = [(b, a) for a, b in self.right]

    def go_right(self, value):
        return lax.ppermute(value, self.axis, self.right)

    def go_left(self, value):
        return lax.ppermute(value, self.axis, self.left)

    def member(self, offset):
        return self.members[offset % self.count]

    def gather(self, block, axis=0, out_type=None):
        count, rows = self.count, block.shape[axis]
        half = rows // 2
        out_type = out_type or block.dtype
        shape = list(block.shape)
        shape[axis] = count * rows
        out = jnp.zeros(shape, out_type)

        def put(out, value, offset, shift=0):
            start = [0] * block.ndim
            start[axis] = self.member(offset) * rows + shift
            return lax.dynamic_update_slice(
                out, value.astype(out_type), start, allow_negative_indices=False
            )

        right = left = block
        put_next = [(block, 0, 0)]
        for hop in range(1, (count - 1) // 2 + 1):
            right, left = yield right, left
            for item in put_next:
                out = put(out, *item)
            right, left, out = lax.optimization_barrier((right, left, out))
            put_next = [(right, -hop, 0), (left, hop, 0)]
        if count % 2 == 0:
            far = count // 2
            near_half = lax.slice_in_dim(right, 0, half, axis=axis)
            far_half = lax.slice_in_dim(left, half, rows, axis=axis)
            right, left = yield near_half, far_half
            put_next += [(right, -far, 0), (left, far, half)]
        for item in put_next:
            out = put(out, *item)
        return out

    def scatter_sum(self, whole, axis=0):
        rows = whole.shape[axis] // self.count
        half = rows // 2
        shape = list(whole.shape)
        blocks = whole.reshape(shape[:axis] + [self.count, rows] + shape[axis + 1 :])
        sizes = shape[:axis] + [1, half] + shape[axis + 1 :]

        def pick(offset, shift):
            start = [0] * blocks.ndim
            start[axis], start[axis + 1] = self.member(offset), shift
            value = lax.dynamic_slice(blocks, start, sizes, allow_negative_indices=False)
            return jnp.squeeze(value, axis)

        right, left = pick(-1, 0), pick(1, half)
        for hop in range(1, self.count):
            right, left = yield right, left
            right = right.astype(f32) + pick(-1 - hop, 0).astype(f32)
            left = left.astype(f32) + pick(1 + hop, half).astype(f32)
            if hop < self.count - 1:
                right, left = right.astype(bf16), left.astype(bf16)
        return right, left

    def sum_all(self, shard):
        halves = yield from self.scatter_sum(shard)
        block = jnp.concatenate([part.astype(bf16) for part in halves], axis=0)
        return (yield from self.gather(block, out_type=f32))

    def run(self, chains):
        results, arrived, token = {}, {}, None
        number = 0
        while len(results) < len(chains):
            turns = max(hops for start, hops, steps in chains)
            for turn in range(turns):
                for k, (start, hops, steps) in enumerate(chains):
                    if k in results or number < start or turn >= hops:
                        continue
                    try:
                        payload = steps.send(arrived.get(k))
                    except StopIteration as stop:
                        results[k] = stop.value
                        continue
                    if token is not None:
                        payload, token = lax.optimization_barrier((payload, token))
                    token = payload[0]
                    arrived[k] = (self.go_right(payload[0]), self.go_left(payload[1]))
            number += 1
        return [results[k] for k in range(len(chains))]


class Cube:
    def __init__(self, axis, count):
        self.axis = axis
        self.count = count
        self.members = table_row(
            [[k ^ key for key in range(count)] for k in range(count)], lax.axis_index(axis)
        )
        self.bits = [1 << k for k in range(count.bit_length() - 1)]

    def swap(self, value, bit):
        return lax.ppermute(value, self.axis, [(k, k ^ bit) for k in range(self.count)])

    def gather(self, shard):
        held = {0: shard}
        for bit in reversed(self.bits):
            held.update({key ^ bit: self.swap(value, bit) for key, value in held.items()})
        rows = shard.shape[0]
        out = jnp.zeros((self.count * rows,) + shard.shape[1:], shard.dtype)
        for key, value in held.items():
            start = (self.members[key] * rows,) + (0,) * (shard.ndim - 1)
            out = lax.dynamic_update_slice(out, value, start, allow_negative_indices=False)
        return out

    def scatter_sum(self, whole):
        blocks = whole.reshape((self.count, whole.shape[0] // self.count) + whole.shape[1:])
        held = {
            key: lax.dynamic_slice(
                blocks,
                (self.members[key],) + (0,) * whole.ndim,
                (1,) + blocks.shape[1:],
                allow_negative_indices=False,
            )[0]
            for key in range(self.count)
        }
        for bit in self.bits:
            far = [key for key in held if key & bit]
            arrived = yield bit, [held.pop(key) for key in far]
            for key, value in zip(far, arrived):
                kept = key ^ bit
                held[kept] = (held[kept].astype(f32) + value.astype(f32)).astype(bf16)
        return held[0]

    def send(self, payload):
        bit, values = payload
        return [self.swap(value, bit) for value in values]

    def finish(self, steps, arrived=None):
        while True:
            try:
                arrived = self.send(steps.send(arrived))
            except StopIteration as stop:
                return stop.value


def layout(lengths, places):
    ends = jnp.cumsum(lengths)
    starts = ends - lengths
    member = jnp.sum((places[:, None] >= ends[None, :]).astype(jnp.int32), axis=1)
    chosen = member[:, None] == jnp.arange(lengths.shape[0], dtype=jnp.int32)[None, :]
    return jnp.sum(jnp.where(chosen, starts[None, :], 0), axis=1)


def body(
    fsdp_count,
    ctx_count,
    tokens,
    seq_lengths,
    attn_gain,
    w_query,
    w_key,
    w_value,
    query_gain,
    key_gain,
    w_output,
    mlp_gain,
    w_gate,
    w_up,
    w_down,
    out_grad,
):
    groups, rows, width = tokens.shape
    total = rows * ctx_count
    flat_rows = groups * rows
    ctx = lax.axis_index("ctx")
    ring, cube = Ring("ctx", ctx_count), Cube("fsdp", fsdp_count)

    query_heads, key_heads = w_query.shape[1] // HD, w_key.shape[1] // HD
    heads = query_heads // ctx_count
    query_width = heads * HD
    shared = ctx_count // key_heads
    key_head = ctx // shared
    w_mine = jnp.concatenate(
        [
            lax.dynamic_slice(w_query, (0, ctx * query_width), (w_query.shape[0], query_width)),
            lax.dynamic_slice(w_key, (0, key_head * HD), (w_key.shape[0], HD)),
            lax.dynamic_slice(w_value, (0, key_head * HD), (w_value.shape[0], HD)),
        ],
        axis=1,
    )
    packed = jnp.concatenate([attn_gain, mlp_gain, query_gain, key_gain])
    all_gains = cube.gather(packed[None, :]).astype(f32)
    d_shard, h_shard = attn_gain.shape[0], query_gain.shape[0]
    gain_attn = all_gains[:, :d_shard].reshape(-1)
    gain_mlp = all_gains[:, d_shard : 2 * d_shard].reshape(-1)
    gain_query = all_gains[:, 2 * d_shard : 2 * d_shard + h_shard].reshape(-1)
    gain_key = all_gains[:, 2 * d_shard + h_shard :].reshape(-1)
    head_gains = jnp.stack([gain_query, gain_key])
    w_heads = cube.gather(w_mine)

    full_output = lax.all_gather(w_output, "fsdp", axis=0, tiled=True)
    full_gate = lax.all_gather(w_gate, "fsdp", axis=0, tiled=True)
    full_up = lax.all_gather(w_up, "fsdp", axis=0, tiled=True)
    full_down = lax.all_gather(w_down, "fsdp", axis=0, tiled=True)

    places = jnp.arange(total, dtype=jnp.int32)
    first = jax.vmap(lambda lengths: layout(lengths, places))(seq_lengths)
    lane = jnp.arange(HD, dtype=jnp.int32)
    inverse = jnp.exp(
        lax.rem(lane, HD // 2).astype(f32) * (-2.0 * math.log(1000000.0) / HD)
    )
    angles = (places[None, :] - first).astype(f32)[:, :, None] * inverse[None, None, :]
    cosine = jnp.cos(angles)
    sine = jnp.sin(angles) * jnp.where(lane < HD // 2, -1.0, 1.0)

    (all_tokens,) = ring.run([(0, 1, ring.gather(tokens, axis=1))])
    group_normed, group_lin, saved, attended = [], [], [], []
    for g in range(groups):
        values = all_tokens[g].astype(f32)
        normed = (values * inverse_rms(values) * gain_attn).astype(bf16)
        lin = matmul(normed, w_heads)
        qkv, att, att_t, lse = attention_forward(
            lin, cosine[g], sine[g], first[g][None, :], head_gains
        )
        back = lax.all_to_all(
            att.reshape(ctx_count, rows, query_width), "ctx", 0, 0, tiled=True
        )
        attended.append(jnp.swapaxes(back, 0, 1).reshape(rows, ctx_count * query_width))
        group_normed.append(normed)
        group_lin.append(lin)
        saved.append((qkv, att_t, lse))

    inputs = tokens.reshape(flat_rows, width).astype(f32)
    cotangent = out_grad.reshape(flat_rows, width)
    earlier, tag = (), att
    group_grad, kept = [], []
    for g in range(groups):
        attended[g], tag = lax.optimization_barrier((attended[g], tag))
        middle = tokens[g].astype(f32) + matmul(attended[g], full_output)
        normed = (middle * inverse_rms(middle) * gain_mlp).astype(bf16)
        *earlier, feed_out, grad_normed = feed_forward(
            g, groups, earlier, normed, out_grad[g], full_gate, full_up, full_down
        )
        grad = out_grad[g].astype(f32) + rms_backward(middle, gain_mlp, grad_normed)
        branch = grad.astype(bf16)
        part = contract_cols(branch, full_output).astype(bf16)
        part = jnp.swapaxes(part.reshape(rows, ctx_count, query_width), 0, 1)
        arrived = lax.all_to_all(part, "ctx", 0, 0, tiled=True)
        group_grad.append(arrived.reshape(total, query_width))
        kept.append((normed, grad, branch, (middle + feed_out).astype(bf16), attended[g]))
        tag = part
    kept, earlier, tag, group_grad[0] = lax.optimization_barrier(
        (kept, tuple(earlier), tag, group_grad[0])
    )
    hidden, grad_gate_low, grad_up_low = earlier
    normed_mlp, grad_middle, grad_branch, output, attended_low = [
        jnp.concatenate(values, axis=0) for values in zip(*kept)
    ]
    shard_down, shard_output, shard_gate, shard_up = [
        lax.psum_scatter(
            contract_rows(left, right).astype(bf16), "fsdp", scatter_dimension=0, tiled=True
        )
        for left, right in (
            (hidden, cotangent),
            (attended_low, grad_branch),
            (normed_mlp, grad_gate_low),
            (normed_mlp, grad_up_low),
        )
    ]

    grad_heads = jnp.zeros(w_heads.shape, f32)
    grad_query_gain = jnp.zeros((1, HD), f32)
    grad_key_gain = jnp.zeros((1, HD), f32)
    group_low, partials = [], []
    for g in range(groups):
        qkv, att_t, lse = saved[g]
        if g + 1 < groups:
            group_grad[g], group_grad[g + 1] = lax.optimization_barrier(
                (group_grad[g], group_grad[g + 1])
            )
        grad_low, query_part, key_part = attention_backward(
            qkv,
            group_lin[g],
            group_grad[g],
            att_t,
            lse,
            cosine[g],
            sine[g],
            first[g][None, :],
            head_gains,
        )
        grad_query_gain = grad_query_gain + query_part
        grad_key_gain = grad_key_gain + key_part
        group_low.append(grad_low)
        partial = contract_cols(grad_low, w_heads).astype(bf16)
        if g + 1 < groups:
            group_grad[g + 1], partial = lax.optimization_barrier((group_grad[g + 1], partial))
        partials.append(partial)
    for g in range(groups):
        grad_heads = grad_heads + contract_rows(group_normed[g], group_low[g])
    partial = jnp.stack(partials)

    small = jnp.concatenate(
        [grad_query_gain.reshape(fsdp_count, h_shard), grad_key_gain.reshape(fsdp_count, h_shard)],
        axis=1,
    )
    small = jnp.pad(small, ((0, 0), (0, d_shard - 2 * h_shard))).reshape(-1, 1)
    small = jnp.pad(small, ((0, 0), (0, HD - 1)))
    mine = cube.finish(
        cube.scatter_sum(jnp.concatenate([grad_heads, small], axis=1).astype(bf16))
    )
    split = shard_down.shape[0]
    shard_rows = jnp.concatenate([shard_down, shard_output], axis=0)
    shard_pair = jnp.concatenate([shard_gate, shard_up], axis=0)
    halves, summed_rows, summed_pair, gathered = ring.run(
        [
            (0, 1, ring.scatter_sum(partial, axis=1)),
            (0, 2, ring.sum_all(shard_rows)),
            (3, 2, ring.sum_all(shard_pair)),
            (4, 2, ring.gather(mine, out_type=f32)),
        ]
    )
    grad_normed = jnp.concatenate(halves, axis=1).reshape(flat_rows, width)
    token_grad = grad_middle + rms_backward(inputs, gain_attn, grad_normed)
    shard_down, shard_output = summed_rows[:split], summed_rows[split:]
    shard_gate, shard_up = summed_pair[:d_shard], summed_pair[d_shard:]
    gathered = gathered.reshape(ctx_count, d_shard, -1)
    shard_query = jnp.swapaxes(gathered[:, :, :query_width], 0, 1).reshape(d_shard, -1)

    def key_columns(start):
        part = gathered[:, :, start : start + HD].reshape(key_heads, shared, d_shard, HD)
        return jnp.swapaxes(jnp.sum(part, axis=1), 0, 1).reshape(d_shard, -1)

    shard_key = key_columns(query_width)
    shard_value = key_columns(query_width + HD)
    head_sums = jnp.sum(gathered[:, : 2 * h_shard, query_width + 2 * HD], axis=0)
    shard_attn_gain = (
        jnp.sum(shard_query * w_query.astype(f32), axis=1)
        + jnp.sum(shard_key * w_key.astype(f32), axis=1)
        + jnp.sum(shard_value * w_value.astype(f32), axis=1)
    ) / attn_gain.astype(f32)
    shard_mlp_gain = (
        jnp.sum(shard_gate * w_gate.astype(f32), axis=1)
        + jnp.sum(shard_up * w_up.astype(f32), axis=1)
    ) / mlp_gain.astype(f32)
    return (
        output.reshape(groups, rows, width),
        token_grad.reshape(groups, rows, width),
        shard_attn_gain,
        shard_query,
        shard_key,
        shard_value,
        head_sums[:h_shard],
        head_sums[h_shard:],
        shard_output,
        shard_mlp_gain,
        shard_gate,
        shard_up,
        shard_down,
    )


def solution(mesh):
    rows, matrix, vector = P("fsdp", "ctx", None), P("fsdp", None), P("fsdp")
    return jax.shard_map(
        functools.partial(body, mesh.shape["fsdp"], mesh.shape["ctx"]),
        mesh=mesh,
        in_specs=(
            rows,
            matrix,
            vector,
            matrix,
            matrix,
            matrix,
            vector,
            vector,
            matrix,
            vector,
            matrix,
            matrix,
            matrix,
            rows,
        ),
        out_specs=(
            rows,
            rows,
            vector,
            matrix,
            matrix,
            matrix,
            vector,
            vector,
            matrix,
            vector,
            matrix,
            matrix,
            matrix,
        ),
        check_vma=False,
    )
```
